256 devices in a mesh: frame: 16 (over y_lo, x, core), seq: 16 (over y_hi, z).
Axes of the slice: x: 4, y: 4 (y_hi: 2, y_lo: 2; y = y_hi * 2 + y_lo), z: 8, core: 2. Of those that a mesh axis runs over, the one named last changes fastest.
Arguments:
- queue_tokens: bfloat16 [16, 640, 3072], P('frame', 'seq'), may hold values from -6 to 6
- timesteps: int32 [16], P('frame'), may hold values from 0 to 991, as said below
- fresh_noise: bfloat16 [640, 3072], P('seq'), may hold values from -6 to 6
- w_mod: bfloat16 [512, 9216], P(None, 'seq'), may hold values from -0.25 to 0.25
- w_qkv: bfloat16 [3072, 3, 2048], P(None, None, 'seq'), may hold values from -0.109375 to 0.109375
- q_gain: float32 [64], replicated, may hold values from 0.9 to 6
- k_gain: float32 [64], replicated, may hold values from 0.9 to 6
- w_out: bfloat16 [2048, 3072], P('seq'), may hold values from -0.75 to 0.75
Outputs:
- queue_next: bfloat16 [16, 640, 3072], P('frame', 'seq')
The draws below stay inside these ranges and needn't reach their ends.
Inputs may be any that keep to these rules, and one draw needn't show every extreme that they name: `timesteps`: slot number s has a level from s * 62 to (s + 1) * 62 - 1, so levels rise strictly along the queue; the first slot has level 0 and the last slot level 991.
All inputs are finite; a program needn't handle non-finite values.
Results may differ from the reference program's by a relative error of at most 0.03.
The reference program's roundings to bfloat16 on the way count: a program that leaves them out, or rounds other values in their place, can miss the bound.
Values may be sent and summed in bfloat16 or wider, within the bound.
A program may use at most 64 MiB of HBM per device.

```python
import math
import jax
import jax.numpy as jnp
from jax import lax

D = 3072
HEAD = 64
TEMB = 512
HEADS = 32
FRAMES = 16
FTOK = 640
INNER = 2048
HEADS_DEV = 2
LEVEL = 62
N_SEQ = 16


def draw_timesteps(key, part):
    key = jax.random.fold_in(key, 3)
    offsets = jax.random.randint(key, (FRAMES,), 0, LEVEL).astype(jnp.int32)
    offsets = offsets.at[0].set(0).at[FRAMES - 1].set(LEVEL - 1)
    return jnp.arange(FRAMES, dtype=jnp.int32) * LEVEL + offsets


def draw_q_gain(key, part):
    key = jax.random.fold_in(key, 1)
    return jax.random.uniform(key, (HEAD,), jnp.float32, 0.9, 2.1)


def draw_k_gain(key, part):
    key = jax.random.fold_in(key, 2)
    return jax.random.uniform(key, (HEAD,), jnp.float32, 0.9, 2.1)


def block_levels(rng, extent, shards, least, high):
    def one(position, shards_of):
        steps = jax.random.uniform(jax.random.fold_in(jax.random.fold_in(rng, 6), position), (shards_of,), jnp.float32, least / len(shards), high / len(shards))
        return jnp.repeat(jnp.exp(steps), extent[position] // shards_of).reshape((-1,) + (1,) * (len(extent) - position - 1))

    loudness = one(*shards[0])
    for cut in shards[1:]:
        loudness = loudness * one(*cut)
    return loudness


def scatter_about(key, dims, scale, bound, split=(), kind=jnp.bfloat16):
    loudness = block_levels(key, dims, split, -0.22, 0.18) if split else 1.0
    result = jax.random.normal(key, dims, jnp.float32) * scale * loudness
    return jnp.minimum(jnp.maximum(result, -bound), bound).astype(kind)


def setup_inputs(seed: int = 0) -> dict:
    streams_of = jax.random.split(jax.random.key(seed), 9)
    return {
        "queue_tokens": scatter_about(streams_of[0], (FRAMES, FTOK, D), 1.0, 6.0, ((0, 16), (1, 16))),
        "timesteps": draw_timesteps(jax.random.fold_in(streams_of[8], 71), 0),
        "fresh_noise": scatter_about(streams_of[2], (FTOK, D), 1.0, 6.0, ((0, 16),)),
        "w_mod": scatter_about(streams_of[3], (TEMB, 3 * D), TEMB ** -0.5, 0.25, ((1, 16),)),
        "w_qkv": scatter_about(streams_of[4], (D, 3, INNER), D ** -0.5, 0.109375, ((2, 16),)),
        "q_gain": draw_q_gain(jax.random.fold_in(streams_of[8], 71), 0),
        "k_gain": draw_k_gain(jax.random.fold_in(streams_of[8], 71), 0),
        "w_out": scatter_about(streams_of[7], (INNER, D), HEAD ** -0.5, 0.75, ((0, 16),)),
    }


def embed_steps(levels):
    halfway = TEMB // 2
    frequency = jnp.exp(-math.log(10000.0) * jnp.arange(halfway, dtype=jnp.float32) / halfway)
    angles = levels.astype(jnp.float32)[:, None] * frequency[None, :]
    return jnp.concatenate([jnp.cos(angles), jnp.sin(angles)], axis=-1)

def head_norm(values, gains):
    average = lax.optimization_barrier(jnp.mean(values, axis=-1, keepdims=True))
    centred = values - average
    spread = lax.optimization_barrier(jnp.mean(centred * centred, axis=-1, keepdims=True))
    return centred * lax.rsqrt(spread + 1e-06) * gains

def modulate(tok_rows, shift_vec, scale_vec):
    widened = tok_rows.astype(jnp.float32)
    average = lax.optimization_barrier(jnp.mean(widened, axis=-1, keepdims=True))
    centred = widened - average
    spread = lax.optimization_barrier(jnp.mean(centred * centred, axis=-1, keepdims=True))
    normed = centred * lax.rsqrt(spread + 1e-05)
    return (normed * (1.0 + scale_vec) + shift_vec).astype(jnp.bfloat16)

def attend(queries, key_rows, value_rows):
    length = queries.shape[0]
    block_len = math.gcd(length, 512)
    head_count = queries.shape[1]
    head_size = queries.shape[2]
    blocks = queries.reshape(length // block_len, block_len, head_count, head_size)
    keys_wide = key_rows.astype(jnp.float32)
    values_wide = value_rows.astype(jnp.float32)

    def one_block(query_block):
        scores = jnp.einsum('qhc,fkhc->hqfk', query_block.astype(jnp.float32), keys_wide) * head_size ** (-0.5)
        highest = lax.optimization_barrier(jnp.max(scores, axis=(2, 3), keepdims=True))
        exponent = jnp.exp(scores - highest)
        summed = lax.optimization_barrier(jnp.sum(exponent, axis=(2, 3), keepdims=True))
        weights = (exponent / summed).astype(jnp.bfloat16)
        mixed = jnp.einsum('hqfk,fkhc->qhc', weights.astype(jnp.float32), values_wide)
        return mixed.astype(jnp.bfloat16).reshape(block_len, head_count * head_size)
    return lax.map(one_block, blocks).reshape(length, head_count * head_size)

def reference(queue_tokens, timesteps, fresh_noise, w_mod, w_qkv, q_gain, k_gain, w_out):
    condition = jax.nn.silu(embed_steps(timesteps)).astype(jnp.bfloat16)
    modulation = jnp.dot(condition, w_mod, preferred_element_type=jnp.float32)
    shifts = modulation[:, :D]
    scales = modulation[:, D:2 * D]
    gates = modulation[:, 2 * D:]
    qkv_matrix = w_qkv.reshape(D, 3 * HEADS * HEAD)

    def project(frame_args):
        tok_rows, shift_vec, scale_vec = frame_args
        modded = modulate(tok_rows, shift_vec, scale_vec)
        joined = jnp.dot(modded, qkv_matrix, preferred_element_type=jnp.float32).reshape(FTOK, 3, HEADS, HEAD)
        normed_q = head_norm(joined[:, 0], q_gain).astype(jnp.bfloat16)
        normed_k = head_norm(joined[:, 1], k_gain).astype(jnp.bfloat16)
        plain_v = joined[:, 2].astype(jnp.bfloat16)
        return (normed_q, normed_k, plain_v)
    queries, keys_all, values_all = lax.map(project, (queue_tokens, shifts, scales))
    group_width = HEADS_DEV * HEAD

    def update(frame_index):
        mixed = attend(queries[frame_index], keys_all, values_all)
        projected = jnp.zeros((FTOK, D), jnp.float32)
        for member in range(N_SEQ):
            partial_value = jnp.dot(mixed[:, member * group_width:(member + 1) * group_width], w_out[member * group_width:(member + 1) * group_width], preferred_element_type=jnp.float32)
            rounded = lax.optimization_barrier(partial_value.astype(jnp.bfloat16))
            projected = projected + rounded.astype(jnp.float32)
        return (queue_tokens[frame_index].astype(jnp.float32) + gates[frame_index] * projected).astype(jnp.bfloat16)
    updated = lax.map(update, jnp.arange(FRAMES, dtype=jnp.int32))
    return jnp.concatenate([updated[1:], fresh_noise[None]], axis=0)
```

```python
import math

import jax
import jax.numpy as jnp
from jax import lax
from jax.experimental import pallas as pl
from jax.experimental.pallas import tpu as pltpu
from jax.sharding import PartitionSpec as P

TEMB = 512
TOK = 40
D = 3072
GROUP = 128
HEAD = 64
BF = jnp.bfloat16
F32 = jnp.float32
MESH = pl.DeviceIdType.MESH
VMEM_LIMIT = 56 * 1024 * 1024


def embed_steps(levels):
    halfway = TEMB // 2
    frequency = jnp.exp(-math.log(10000.0) * jnp.arange(halfway, dtype=F32) / halfway)
    angles = levels.astype(F32)[:, None] * frequency[None, :]
    return jnp.concatenate([jnp.cos(angles), jnp.sin(angles)], axis=-1)


class Place:
    def __init__(self):
        f = lax.axis_index("frame")
        s = lax.axis_index("seq")
        self.f, self.s = f, s
        ylo, x, core = f // 8, (f // 2) % 4, f % 2
        yhi, z = s // 8, s % 8

        def frame(yl, xx, cc):
            return yl * 8 + xx * 2 + cc

        self.sib = (frame(ylo, x, 1 - core), s)
        self.ylo = (frame(1 - ylo, x, core), s)
        self.xp = (frame(ylo, (x + 1) % 4, core), s)
        self.xm = (frame(ylo, (x + 3) % 4, core), s)
        self.zp = (f, yhi * 8 + (z + 1) % 8)
        self.zm = (f, yhi * 8 + (z + 7) % 8)
        self.yhi = (f, (1 - yhi) * 8 + z)
        self.prev = ((f + 15) % 16, s)
        self.next = ((f + 1) % 16, s)
        self.at = frame
        self.coords = (ylo, x, core)

    def frame_at(self, dy, dx, dc):
        ylo, x, core = self.coords
        return self.at((ylo + dy) % 2, (x + dx) % 4, (core + dc) % 2)


class Link:
    def __init__(self, send_sem, recv_sem):
        self.send_sem, self.recv_sem = send_sem, recv_sem
        self.sent = []

    def _copy(self, i, src, dst, dev):
        return pltpu.make_async_remote_copy(
            src_ref=src,
            dst_ref=dst,
            send_sem=self.send_sem.at[i],
            recv_sem=self.recv_sem.at[i],
            device_id=dev,
            device_id_type=MESH,
        )

    def send(self, i, src, dst, dev):
        copy = self._copy(i, src, dst, dev)
        copy.start()
        self.sent.append(copy)

    def wait(self, i, dst, dev):
        self._copy(i, dst, dst, dev).wait_recv()

    def drain(self):
        for copy in self.sent:
            copy.wait_send()


def meet(devices):
    barrier = pltpu.get_barrier_semaphore()
    for dev in devices:
        pl.semaphore_signal(barrier, inc=1, device_id=dev, device_id_type=MESH)
    return lambda: pl.semaphore_wait(barrier, len(devices))


def to_block(rows):
    pieces = []
    for h in range(2):
        lo = rows[:, h * 1536 : h * 1536 + 768]
        hi = rows[:, h * 1536 + 768 : (h + 1) * 1536]
        pieces.append(jnp.concatenate([lo, hi], axis=0))
    return pieces


def head_norm_pair(x, gain, first):
    a = jnp.sum(jnp.where(first, x, 0.0), axis=-1, keepdims=True) * (1.0 / HEAD)
    b = jnp.sum(jnp.where(first, 0.0, x), axis=-1, keepdims=True) * (1.0 / HEAD)
    c = x - jnp.where(first, a, b)
    sq = c * c
    va = jnp.sum(jnp.where(first, sq, 0.0), axis=-1, keepdims=True) * (1.0 / HEAD)
    vb = jnp.sum(jnp.where(first, 0.0, sq), axis=-1, keepdims=True) * (1.0 / HEAD)
    return c * lax.rsqrt(jnp.where(first, va, vb) + 1e-06) * gain


def qkv_kernel(
    tok_ref, mod_ref, w_ref, wo_ref, qg_ref, kg_ref,
    q_out, kv_out, wop_out, gate_out,
    blocks, modbuf, modrows, modt, wp, wop, x_scr, swap_out, swap_in,
    send_sem, recv_sem,
):
    here = Place()
    f, s = here.f, here.s
    seq_peers = [(f, lax.rem(s + d, 16)) for d in range(1, 16)]
    ready = meet(seq_peers + [here.sib, here.ylo, here.xp, here.xm])
    link = Link(send_sem, recv_sem)

    tok = tok_ref[...].astype(F32)
    for h, piece in enumerate(to_block(tok)):
        blocks[0, h] = piece.astype(BF)
    modbuf[s] = mod_ref[...]
    ready()

    link.send(0, blocks.at[0], blocks.at[1], here.zp)
    link.send(1, blocks.at[0], blocks.at[2], here.zm)
    for d, dev in enumerate(seq_peers):
        link.send(10 + d, modbuf.at[s], modbuf.at[s], dev)

    def wo_part(i):
        rows = pl.ds(pl.multiple_of((i // 2) * 16, 16), 16)
        cols = pl.ds(pl.multiple_of((i % 2) * 1536, 1536), 1536)
        return wo_ref.at[rows, cols]

    def wop_part(i):
        return wop.at[i // 2, i % 2]

    link.send(25, w_ref.at[f], wp.at[f], here.yhi)
    link.send(26, wo_part(f), wop_part(f), here.yhi)

    def send_w(i, who, dev):
        link.send(i, wp.at[who], wp.at[who], dev)
        link.send(i + 1, wop_part(who), wop_part(who), dev)

    def wait_w(i, who, dev):
        link.wait(i, wp.at[who], dev)
        link.wait(i + 1, wop_part(who), dev)

    def half_w(i, who, half, dev, go):
        a = wp.at[who, pl.ds(96 * half, 96)]
        if go:
            link.send(i, a, a, dev)
        else:
            link.wait(i, a, dev)

    def half_wo(i, who, half, dev, go):
        b = wop.at[who // 2, who % 2, :, pl.ds(768 * half, 768)]
        if go:
            link.send(i, b, b, dev)
        else:
            link.wait(i, b, dev)

    def spread(base, dy):
        who = here.frame_at(dy, 0, 0)
        send_w(base, who, here.xp)
        send_w(base + 2, who, here.xm)
        send_w(base + 4, who, here.sib)

    def relay(base, dy):
        left, right = here.frame_at(dy, 3, 0), here.frame_at(dy, 1, 0)
        wait_w(base, left, here.xm)
        half_w(base + 6, left, 0, here.xp, True)
        half_wo(base + 7, left, 0, here.xp, True)
        send_w(base + 10, left, here.sib)
        wait_w(base + 2, right, here.xp)
        half_w(base + 8, right, 1, here.xm, True)
        half_wo(base + 9, right, 1, here.xm, True)
        send_w(base + 12, right, here.sib)

    def finish(base, dy):
        far = here.frame_at(dy, 2, 0)
        half_w(base + 6, far, 0, here.xm, False)
        half_wo(base + 7, far, 0, here.xm, False)
        half_w(base + 8, far, 1, here.xp, False)
        half_wo(base + 9, far, 1, here.xp, False)
        send_w(base + 14, far, here.sib)

    def sib_all(base, dy):
        wait_w(base + 4, here.frame_at(dy, 0, 1), here.sib)
        wait_w(base + 10, here.frame_at(dy, 3, 1), here.sib)
        wait_w(base + 12, here.frame_at(dy, 1, 1), here.sib)
        wait_w(base + 14, here.frame_at(dy, 2, 1), here.sib)

    W0, W1 = 30, 46
    wait_w(25, f, here.yhi)
    send_w(27, f, here.ylo)
    spread(W0, 0)

    for d in range(1, 16):
        peer = lax.rem(s + 16 - d, 16)
        link.wait(9 + d, modbuf.at[peer], (f, peer))
    for i in range(16):
        modrows[pl.ds(i * 9, 9), :] = modbuf[i, 0:9, :]
    even = modrows[pl.ds(0, 72, stride=2), :]
    odd = modrows[pl.ds(1, 72, stride=2), :]
    modt[...] = jnp.concatenate([even, odd], axis=1)
    gate_out[...] = modt[48:72, :]

    first = lax.broadcasted_iota(jnp.int32, (80, GROUP), 1) < HEAD
    q_scale = math.log2(math.e) / math.sqrt(HEAD)

    def normalise(raw):
        def tile(h, c):
            return raw[h, :, c * 128 : (c + 1) * 128].astype(F32)

        spots = [(h, c) for h in range(2) for c in range(6)]
        total = jnp.zeros((80, 128), F32)
        for h, c in spots:
            total = total + tile(h, c)
        mean = jnp.sum(total[:40] + total[40:], axis=-1, keepdims=True) * (1.0 / D)
        mean = jnp.concatenate([mean, mean], axis=0)
        total = jnp.zeros((80, 128), F32)
        for h, c in spots:
            diff = tile(h, c) - mean
            total = total + diff * diff
        var = jnp.sum(total[:40] + total[40:], axis=-1, keepdims=True) * (1.0 / D)
        inv = lax.rsqrt(var + 1e-05)
        inv = jnp.concatenate([inv, inv], axis=0)
        return lambda h, c: (tile(h, c) - mean) * inv

    def modulate(p, a, b):
        na, nb = normalise(blocks.at[a]), normalise(blocks.at[b])
        for h in range(2):
            for c in range(6):
                va, vb = na(h, c), nb(h, c)
                for half in range(2):
                    t = h * 12 + half * 6 + c
                    rows = slice(half * 40, half * 40 + 40)
                    both = jnp.concatenate([va[rows], vb[rows]], axis=0)
                    scale = 1.0 + modt[24 + t : 25 + t, :]
                    out = both * scale + modt[t : t + 1, :]
                    x_scr[p, t // 6, :, (t % 6) * 128 : (t % 6 + 1) * 128] = out.astype(BF)

    def project(p, weights):
        def step(k, acc):
            part = weights[pl.ds(k * 4, 4)].reshape(768, 3 * GROUP)
            return acc + jnp.dot(x_scr[p, k], part, preferred_element_type=F32)

        joined = lax.fori_loop(0, 4, step, jnp.zeros((80, 3 * GROUP), F32))
        q = head_norm_pair(joined[:, :GROUP], qg_ref[...], first) * q_scale
        k = head_norm_pair(joined[:, GROUP : 2 * GROUP], kg_ref[...], first)
        return q.astype(BF), k.astype(BF), joined[:, 2 * GROUP :].astype(BF)

    def project_own(p):
        rows = slice(p * 80, p * 80 + 80)
        q, k, v = project(p, w_ref)
        q_out[rows, :] = q
        kv_out[0, rows, :] = k
        kv_out[1, rows, :] = v

    def project_swap(p):
        q, k, v = project(p, wp)
        rows = slice(p * 80, p * 80 + 80)
        swap_out[0, rows, :] = q
        swap_out[1, rows, :] = k
        swap_out[2, rows, :] = v
        part = pl.ds(p * 80, 80)
        link.send(64 + p, swap_out.at[:, part], swap_in.at[:, part], here.yhi)

    link.wait(0, blocks.at[1], here.zm)
    link.send(2, blocks.at[1], blocks.at[3], here.zp)
    link.wait(1, blocks.at[2], here.zp)
    link.send(3, blocks.at[2], blocks.at[4], here.zm)
    wait_w(27, here.frame_at(1, 0, 0), here.ylo)
    spread(W1, 1)
    modulate(1, 1, 2)
    relay(W0, 0)
    project_own(1)

    link.wait(2, blocks.at[3], here.zm)
    link.send(4, blocks.at[3], blocks.at[5], here.zp)
    link.wait(3, blocks.at[4], here.zp)
    link.send(5, blocks.at[4], blocks.at[6], here.zm)
    relay(W1, 1)
    modulate(2, 3, 4)
    project_own(2)
    finish(W0, 0)

    link.wait(4, blocks.at[5], here.zm)
    link.send(6, blocks.at[5, 0], blocks.at[7, 0], here.zp)
    link.wait(5, blocks.at[6], here.zp)
    link.send(7, blocks.at[6, 1], blocks.at[7, 1], here.zm)
    finish(W1, 1)
    modulate(3, 5, 6)
    project_own(3)
    sib_all(W0, 0)
    sib_all(W1, 1)
    for p in (1, 2, 3):
        project_swap(p)
    link.wait(6, blocks.at[7, 0], here.zm)
    link.wait(7, blocks.at[7, 1], here.zp)
    modulate(0, 0, 7)
    project_swap(0)
    project_own(0)
    wop_out[...] = wop[...]
    for p in (1, 2, 3, 0):
        part = pl.ds(p * 80, 80)
        link.wait(64 + p, swap_in.at[:, part], here.yhi)
    q_out[320:640, :] = swap_in[0]
    kv_out[0, 320:640, :] = swap_in[1]
    kv_out[1, 320:640, :] = swap_in[2]
    link.drain()


def qkv_call(tok, mod, w, wo, qg, kg):
    vm = pl.BlockSpec(memory_space=pltpu.VMEM)
    return pl.pallas_call(
        qkv_kernel,
        out_shape=(
            jax.ShapeDtypeStruct((640, GROUP), BF),
            jax.ShapeDtypeStruct((2, 640, GROUP), BF),
            jax.ShapeDtypeStruct((8, 2, 16, 1536), BF),
            jax.ShapeDtypeStruct((24, 128), F32),
        ),
        in_specs=[vm] * 6,
        out_specs=(vm,) * 4,
        scratch_shapes=[
            pltpu.VMEM((8, 2, 80, 768), BF),
            pltpu.VMEM((16, 16, 64), F32),
            pltpu.VMEM((144, 64), F32),
            pltpu.VMEM((72, 128), F32),
            pltpu.VMEM((16, 192, 3 * GROUP), BF),
            pltpu.VMEM((8, 2, 16, 1536), BF),
            pltpu.VMEM((4, 4, 80, 768), BF),
            pltpu.VMEM((3, 320, GROUP), BF),
            pltpu.VMEM((3, 320, GROUP), BF),
            pltpu.SemaphoreType.DMA((68,)),
            pltpu.SemaphoreType.DMA((68,)),
        ],
        compiler_params=pltpu.CompilerParams(
            collective_id=0, has_side_effects=True, vmem_limit_bytes=VMEM_LIMIT
        ),
        name="qkv",
    )(tok, mod, w, wo, qg, kg)


def attend_kernel(q_ref, kv_ref, mixed_out, kv, qm, v2, acc, top, send_sem, recv_sem):
    here = Place()
    ready = meet([here.sib, here.ylo, here.xp, here.xm])
    link = Link(send_sem, recv_sem)
    kv[0] = kv_ref[...]
    lanes = lax.broadcasted_iota(jnp.int32, (640, GROUP), 1) < HEAD
    zero = jnp.zeros((640, GROUP), BF)
    qm[0] = jnp.where(lanes, q_ref[...], zero)
    qm[1] = jnp.where(lanes, zero, q_ref[...])
    acc[...] = jnp.zeros(acc.shape, F32)
    top[...] = jnp.full(top.shape, -1e30, F32)
    ready()

    R = 320

    def attend(slot):
        values = kv[slot, 1]
        one = jnp.ones((640, GROUP), BF)
        v2[0] = jnp.where(lanes, values, one)
        v2[1] = jnp.where(lanes, one, values)

        def step(i, carry):
            h, rows = i // (640 // R), pl.ds(pl.multiple_of((i % (640 // R)) * R, R), R)
            scores = lax.dot_general(
                qm[h, rows, :], kv[slot, 0], (((1,), (1,)), ((), ())),
                preferred_element_type=F32,
            )
            old = top[h, rows, :]
            new = jnp.maximum(old, jnp.max(scores, axis=1, keepdims=True))
            probs = jnp.exp2(scores - jnp.concatenate([new] * 5, axis=1)).astype(BF)
            part = jnp.dot(probs, v2[h], preferred_element_type=F32)
            acc[h, rows, :] = acc[h, rows, :] * jnp.exp2(old - new) + part
            top[h, rows, :] = new
            return carry

        lax.fori_loop(0, 2 * (640 // R), step, 0)

    def spread(base, slot):
        link.send(base, kv.at[slot], kv.at[slot + 1], here.xp)
        link.send(base + 1, kv.at[slot], kv.at[slot + 2], here.xm)
        link.send(base + 2, kv.at[slot], kv.at[slot + 8], here.sib)

    def relay(base, slot):
        link.wait(base, kv.at[slot + 1], here.xm)
        link.send(base + 3, kv.at[slot + 1, 0], kv.at[slot + 3, 0], here.xp)
        link.send(base + 5, kv.at[slot + 1], kv.at[slot + 9], here.sib)
        link.wait(base + 1, kv.at[slot + 2], here.xp)
        link.send(base + 4, kv.at[slot + 2, 1], kv.at[slot + 3, 1], here.xm)
        link.send(base + 6, kv.at[slot + 2], kv.at[slot + 10], here.sib)

    def finish(base, slot):
        link.wait(base + 3, kv.at[slot + 3, 0], here.xm)
        link.wait(base + 4, kv.at[slot + 3, 1], here.xp)
        link.send(base + 7, kv.at[slot + 3], kv.at[slot + 11], here.sib)

    def from_sib(i, slot):
        link.wait(i, kv.at[slot], here.sib)
        attend(slot)

    link.send(16, kv.at[0], kv.at[4], here.ylo)
    spread(0, 0)
    attend(0)
    from_sib(2, 8)
    link.wait(16, kv.at[4], here.ylo)
    spread(8, 4)
    attend(4)
    relay(0, 0)
    attend(1)
    attend(2)
    from_sib(10, 12)
    relay(8, 4)
    from_sib(5, 9)
    finish(0, 0)
    from_sib(6, 10)
    attend(3)
    attend(5)
    finish(8, 4)
    attend(6)
    from_sib(13, 13)
    from_sib(14, 14)
    from_sib(7, 11)
    attend(7)
    from_sib(15, 15)

    top_half = acc[0] / pltpu.roll(acc[0], HEAD, 1)
    low_half = acc[1] / pltpu.roll(acc[1], HEAD, 1)
    mixed_out[...] = jnp.where(lanes, top_half, low_half).astype(BF)
    link.drain()


def attend_call(q, kv):
    vm = pl.BlockSpec(memory_space=pltpu.VMEM)
    return pl.pallas_call(
        attend_kernel,
        out_shape=jax.ShapeDtypeStruct((640, GROUP), BF),
        in_specs=[vm] * 2,
        out_specs=vm,
        scratch_shapes=[
            pltpu.VMEM((16, 2, 640, GROUP), BF),
            pltpu.VMEM((2, 640, GROUP), BF),
            pltpu.VMEM((2, 640, GROUP), BF),
            pltpu.VMEM((2, 640, GROUP), F32),
            pltpu.VMEM((2, 640, GROUP), F32),
            pltpu.SemaphoreType.DMA((17,)),
            pltpu.SemaphoreType.DMA((17,)),
        ],
        compiler_params=pltpu.CompilerParams(
            collective_id=1, has_side_effects=True, vmem_limit_bytes=VMEM_LIMIT
        ),
        name="attend",
    )(q, kv)


def out_kernel(
    mixed_ref, wo_ref, wop_ref, tok_ref, gate_ref, fresh_ref,
    out_ref,
    w2, lhs, other, part, up, down, up_in, down_in, moved, arrived,
    send_sem, recv_sem,
):
    here = Place()
    ready = meet([here.yhi, here.zp, here.zm, here.prev, here.next])
    link = Link(send_sem, recv_sem)
    lhs[:, :GROUP] = mixed_ref[0:320, :]
    ready()
    link.send(0, mixed_ref.at[pl.ds(320, 320)], other, here.yhi)
    w2[0:128, :] = wo_ref[...]
    for h in range(2):
        w2[128:256, h * 1536 : (h + 1) * 1536] = wop_ref[:, h].reshape(128, 1536)
    link.wait(0, other, here.yhi)
    lhs[:, GROUP:] = other[...]

    def multiply(p):
        for h in range(2):
            sums = []
            for k in range(2):
                c = h * 1536 + k * 768
                sums.append(
                    jnp.dot(
                        lhs[p * 80 : p * 80 + 80, :], w2[:, c : c + 768],
                        preferred_element_type=F32,
                    )
                )
            part[0, h] = jnp.concatenate([sums[0][:40], sums[1][:40]], axis=0)
            part[1, h] = jnp.concatenate([sums[0][40:], sums[1][40:]], axis=0)

    multiply(0)
    down[0, 0] = part[1, 0].astype(BF)
    link.send(1, down.at[0, 0], down_in.at[0, 0], here.zm)
    up[0, 1] = part[1, 1].astype(BF)
    link.send(2, up.at[0, 1], up_in.at[0, 1], here.zp)
    own = [part[0, h] for h in range(2)]
    for h in range(2):
        moved[h] = own[h]

    for step, p in ((1, 3), (2, 2), (3, 1)):
        multiply(p)
        for h in ((0, 1) if step > 1 else (1, 0)):
            i = 1 + 4 * step + 2 * h
            if step == 1:
                if h == 0:
                    link.wait(1, down_in.at[0, 0], here.zp)
                else:
                    link.wait(2, up_in.at[0, 1], here.zm)
            else:
                link.wait(i - 4, down_in.at[step - 1, h], here.zp)
                link.wait(i - 3, up_in.at[step - 1, h], here.zm)
            low, high = part[0, h], part[1, h]
            if step > 1 or h == 0:
                low = low + down_in[step - 1, h].astype(F32)
            if step > 1 or h == 1:
                high = high + up_in[step - 1, h].astype(F32)
            down[step, h] = low.astype(BF)
            link.send(i, down.at[step, h], down_in.at[step, h], here.zm)
            up[step, h] = high.astype(BF)
            link.send(i + 1, up.at[step, h], up_in.at[step, h], here.zp)

    tok = to_block(tok_ref[...].astype(F32))
    for h in range(2):
        i = 13 + 2 * h
        link.wait(i, down_in.at[3, h], here.zp)
        link.wait(i + 1, up_in.at[3, h], here.zm)
        total = moved[h] + down_in[3, h].astype(F32) + up_in[3, h].astype(F32)
        pieces = []
        for c in range(6):
            cols = slice(c * 128, (c + 1) * 128)
            t = h * 12 + c
            lo = total[:40, cols] * gate_ref[t : t + 1, :]
            hi = total[40:, cols] * gate_ref[t + 6 : t + 7, :]
            pieces.append(jnp.concatenate([lo, hi], axis=0))
        arrived[0, h] = (tok[h] + jnp.concatenate(pieces, axis=1)).astype(BF)
        link.send(17 + h, arrived.at[0, h], arrived.at[1, h], here.prev)
    last = here.f == 15
    fresh = fresh_ref[...].astype(F32)
    for h in range(2):
        link.wait(17 + h, arrived.at[1, h], here.next)
        got = arrived[1, h].astype(F32)
        for k in range(2):
            cols = slice(h * 1536 + k * 768, h * 1536 + (k + 1) * 768)
            out_ref[:, cols] = jnp.where(last, fresh[:, cols], got[k * 40 : k * 40 + 40]).astype(BF)
    link.drain()


def out_call(mixed, wo, wop, tok, gate, fresh):
    vm = pl.BlockSpec(memory_space=pltpu.VMEM)
    blk = (4, 2, 80, 768)
    return pl.pallas_call(
        out_kernel,
        out_shape=jax.ShapeDtypeStruct((TOK, D), BF),
        in_specs=[vm] * 6,
        out_specs=vm,
        scratch_shapes=[
            pltpu.VMEM((256, D), BF),
            pltpu.VMEM((320, 256), BF),
            pltpu.VMEM((320, GROUP), BF),
            pltpu.VMEM((2, 2, 80, 768), F32),
            pltpu.VMEM(blk, BF),
            pltpu.VMEM(blk, BF),
            pltpu.VMEM(blk, BF),
            pltpu.VMEM(blk, BF),
            pltpu.VMEM((2, 80, 768), F32),
            pltpu.VMEM((2, 2, 80, 768), BF),
            pltpu.SemaphoreType.DMA((19,)),
            pltpu.SemaphoreType.DMA((19,)),
        ],
        compiler_params=pltpu.CompilerParams(
            collective_id=2, has_side_effects=True, vmem_limit_bytes=VMEM_LIMIT
        ),
        name="out",
    )(mixed, wo, wop, tok, gate, fresh)


def body(queue_tokens, timesteps, fresh_noise, w_mod, w_qkv, q_gain, k_gain, w_out):
    tok = queue_tokens[0]
    condition = jax.nn.silu(embed_steps(timesteps)).astype(BF)
    own = jnp.dot(condition, w_mod, preferred_element_type=F32)
    mod = jnp.pad(own.reshape(9, 64), ((0, 7), (0, 0)))
    w = w_qkv.reshape(16, 192, 3 * GROUP)
    qg = jnp.concatenate([q_gain, q_gain])[None]
    kg = jnp.concatenate([k_gain, k_gain])[None]
    q, kv, wop, gate = qkv_call(tok, mod, w, w_out, qg, kg)
    mixed = attend_call(q, kv)
    return out_call(mixed, w_out, wop, tok, gate, fresh_noise)[None]


def solution(mesh):
    return jax.shard_map(
        body,
        mesh=mesh,
        in_specs=(
            P("frame", "seq", None),
            P("frame"),
            P("seq", None),
            P(None, "seq"),
            P(None, None, "seq"),
            P(),
            P(),
            P("seq", None),
        ),
        out_specs=P("frame", "seq", None),
        check_vma=False,
    )
```

```python
import math

import jax
import jax.numpy as jnp
from jax import lax
from jax.experimental import pallas as pl
from jax.experimental.pallas import tpu as pltpu
from jax.sharding import PartitionSpec as P

TEMB = 512
TOK = 40
D = 3072
GROUP = 128
HEAD = 64
BF = jnp.bfloat16
F32 = jnp.float32
MESH = pl.DeviceIdType.MESH
VMEM_LIMIT = 56 * 1024 * 1024


def embed_steps(levels):
    halfway = TEMB // 2
    frequency = jnp.exp(-math.log(10000.0) * jnp.arange(halfway, dtype=F32) / halfway)
    angles = levels.astype(F32)[:, None] * frequency[None, :]
    return jnp.concatenate([jnp.cos(angles), jnp.sin(angles)], axis=-1)


class Place:
    def __init__(self):
        f = lax.axis_index("frame")
        s = lax.axis_index("seq")
        self.f, self.s = f, s
        ylo, x, core = f // 8, (f // 2) % 4, f % 2
        yhi, z = s // 8, s % 8

        def frame(yl, xx, cc):
            return yl * 8 + xx * 2 + cc

        self.sib = (frame(ylo, x, 1 - core), s)
        self.ylo = (frame(1 - ylo, x, core), s)
        self.xp = (frame(ylo, (x + 1) % 4, core), s)
        self.xm = (frame(ylo, (x + 3) % 4, core), s)
        self.zp = (f, yhi * 8 + (z + 1) % 8)
        self.zm = (f, yhi * 8 + (z + 7) % 8)
        self.yhi = (f, (1 - yhi) * 8 + z)
        self.prev = ((f + 15) % 16, s)
        self.next = ((f + 1) % 16, s)
        self.at = frame
        self.coords = (ylo, x, core)

    def frame_at(self, dy, dx, dc):
        ylo, x, core = self.coords
        return self.at((ylo + dy) % 2, (x + dx) % 4, (core + dc) % 2)


class Link:
    def __init__(self, send_sem, recv_sem):
        self.send_sem, self.recv_sem = send_sem, recv_sem
        self.sent = []

    def _copy(self, i, src, dst, dev):
        src, dst = (ref() if callable(ref) else ref for ref in (src, dst))
        return pltpu.make_async_remote_copy(
            src_ref=src,
            dst_ref=dst,
            send_sem=self.send_sem.at[i],
            recv_sem=self.recv_sem.at[i],
            device_id=dev,
            device_id_type=MESH,
        )

    def send(self, i, src, dst, dev):
        self._copy(i, src, dst, dev).start()
        self.sent.append((i, src, dst, dev))

    def wait(self, i, dst, dev):
        self._copy(i, dst, dst, dev).wait_recv()

    def drain(self):
        for sent in self.sent:
            self._copy(*sent).wait_send()


def meet(devices):
    barrier = pltpu.get_barrier_semaphore()
    for dev in devices:
        pl.semaphore_signal(barrier, inc=1, device_id=dev, device_id_type=MESH)
    return lambda: pl.semaphore_wait(barrier, len(devices))


def to_block(rows):
    pieces = []
    for h in range(2):
        lo = rows[:, h * 1536 : h * 1536 + 768]
        hi = rows[:, h * 1536 + 768 : (h + 1) * 1536]
        pieces.append(jnp.concatenate([lo, hi], axis=0))
    return pieces


def head_norm_pair(x, gain, first):
    a = jnp.sum(jnp.where(first, x, 0.0), axis=-1, keepdims=True) * (1.0 / HEAD)
    b = jnp.sum(jnp.where(first, 0.0, x), axis=-1, keepdims=True) * (1.0 / HEAD)
    c = x - jnp.where(first, a, b)
    sq = c * c
    va = jnp.sum(jnp.where(first, sq, 0.0), axis=-1, keepdims=True) * (1.0 / HEAD)
    vb = jnp.sum(jnp.where(first, 0.0, sq), axis=-1, keepdims=True) * (1.0 / HEAD)
    return c * lax.rsqrt(jnp.where(first, va, vb) + 1e-06) * gain


def qkv_kernel(
    tok_ref, mod_ref, w_ref, wo_ref, qg_ref, kg_ref,
    q_out, kv_out, wop_out, gate_out,
    blocks, modbuf, modrows, modt, wp, wop, x_scr, swap_out, swap_in,
    send_sem, recv_sem,
):
    here = Place()
    f, s = here.f, here.s
    seq_peers = [(f, lax.rem(s + d, 16)) for d in range(1, 16)]
    ready = meet(seq_peers + [here.sib, here.ylo, here.xp, here.xm])
    link = Link(send_sem, recv_sem)

    tok = tok_ref[...].astype(F32)
    for h, piece in enumerate(to_block(tok)):
        blocks[0, h] = piece.astype(BF)
    modbuf[s] = mod_ref[...]
    ready()

    link.send(0, blocks.at[0], blocks.at[1], here.zp)
    link.send(1, blocks.at[0], blocks.at[2], here.zm)
    for d, dev in enumerate(seq_peers):
        link.send(10 + d, modbuf.at[s], modbuf.at[s], dev)

    def wo_part(i):
        rows = pl.ds(pl.multiple_of((i // 2) * 16, 16), 16)
        cols = pl.ds(pl.multiple_of((i % 2) * 1536, 1536), 1536)
        return wo_ref.at[rows, cols]

    def wop_part(i):
        return wop.at[i // 2, i % 2]

    link.send(25, w_ref.at[:, f], wp.at[:, f], here.yhi)
    link.send(26, wo_part(f), wop_part(f), here.yhi)

    def send_w(i, who, dev):
        link.send(i, wp.at[:, who], wp.at[:, who], dev)
        link.send(i + 1, wop_part(who), wop_part(who), dev)

    def wait_w(i, who, dev):
        link.wait(i, wp.at[:, who], dev)
        link.wait(i + 1, wop_part(who), dev)

    def half_w(i, who, half, dev, go):
        a = wp.at[:, who, pl.ds(96 * half, 96)]
        if go:
            link.send(i, a, a, dev)
        else:
            link.wait(i, a, dev)

    def half_wo(i, who, half, dev, go):
        b = wop.at[who // 2, who % 2, :, pl.ds(768 * half, 768)]
        if go:
            link.send(i, b, b, dev)
        else:
            link.wait(i, b, dev)

    def spread(base, dy):
        who = here.frame_at(dy, 0, 0)
        send_w(base, who, here.xp)
        send_w(base + 2, who, here.xm)
        send_w(base + 4, who, here.sib)

    def relay(base, dy):
        left, right = here.frame_at(dy, 3, 0), here.frame_at(dy, 1, 0)
        wait_w(base, left, here.xm)
        half_w(base + 6, left, 0, here.xp, True)
        half_wo(base + 7, left, 0, here.xp, True)
        send_w(base + 10, left, here.sib)
        wait_w(base + 2, right, here.xp)
        half_w(base + 8, right, 1, here.xm, True)
        half_wo(base + 9, right, 1, here.xm, True)
        send_w(base + 12, right, here.sib)

    def finish(base, dy):
        far = here.frame_at(dy, 2, 0)
        half_w(base + 6, far, 0, here.xm, False)
        half_wo(base + 7, far, 0, here.xm, False)
        half_w(base + 8, far, 1, here.xp, False)
        half_wo(base + 9, far, 1, here.xp, False)
        send_w(base + 14, far, here.sib)

    def sib_all(base, dy):
        wait_w(base + 4, here.frame_at(dy, 0, 1), here.sib)
        wait_w(base + 10, here.frame_at(dy, 3, 1), here.sib)
        wait_w(base + 12, here.frame_at(dy, 1, 1), here.sib)
        wait_w(base + 14, here.frame_at(dy, 2, 1), here.sib)

    W0, W1 = 30, 46
    wait_w(25, f, here.yhi)
    send_w(27, f, here.ylo)
    spread(W0, 0)

    for d in range(1, 16):
        peer = lax.rem(s + 16 - d, 16)
        link.wait(9 + d, modbuf.at[peer], (f, peer))
    for i in range(16):
        modrows[pl.ds(i * 9, 9), :] = modbuf[i, 0:9, :]
    even = modrows[pl.ds(0, 72, stride=2), :]
    odd = modrows[pl.ds(1, 72, stride=2), :]
    modt[...] = jnp.concatenate([even, odd], axis=1)
    gate_out[...] = modt[48:72, :]

    first = lax.broadcasted_iota(jnp.int32, (80, GROUP), 1) < HEAD
    q_scale = math.log2(math.e) / math.sqrt(HEAD)

    def normalise(raw):
        def tile(h, c):
            return raw[h, :, c * 128 : (c + 1) * 128].astype(F32)

        spots = [(h, c) for h in range(2) for c in range(6)]
        total = jnp.zeros((80, 128), F32)
        for h, c in spots:
            total = total + tile(h, c)
        mean = jnp.sum(total[:40] + total[40:], axis=-1, keepdims=True) * (1.0 / D)
        mean = jnp.concatenate([mean, mean], axis=0)
        total = jnp.zeros((80, 128), F32)
        for h, c in spots:
            diff = tile(h, c) - mean
            total = total + diff * diff
        var = jnp.sum(total[:40] + total[40:], axis=-1, keepdims=True) * (1.0 / D)
        inv = lax.rsqrt(var + 1e-05)
        inv = jnp.concatenate([inv, inv], axis=0)
        return lambda h, c: (tile(h, c) - mean) * inv

    def modulate(p, a, b):
        na, nb = normalise(blocks.at[a]), normalise(blocks.at[b])
        for h in range(2):
            for c in range(6):
                va, vb = na(h, c), nb(h, c)
                for half in range(2):
                    t = h * 12 + half * 6 + c
                    rows = slice(half * 40, half * 40 + 40)
                    both = jnp.concatenate([va[rows], vb[rows]], axis=0)
                    scale = 1.0 + modt[24 + t : 25 + t, :]
                    out = both * scale + modt[t : t + 1, :]
                    x_scr[p, t // 6, :, (t % 6) * 128 : (t % 6 + 1) * 128] = out.astype(BF)

    def project(p, weights):
        def step(k, acc):
            part = jnp.concatenate(
                [weights[j, pl.ds(k * 4, 4)].reshape(768, GROUP) for j in range(3)], axis=1
            )
            return acc + jnp.dot(x_scr[p, k], part, preferred_element_type=F32)

        joined = lax.fori_loop(0, 4, step, jnp.zeros((80, 3 * GROUP), F32))
        q = head_norm_pair(joined[:, :GROUP], qg_ref[...], first) * q_scale
        k = head_norm_pair(joined[:, GROUP : 2 * GROUP], kg_ref[...], first)
        return q.astype(BF), k.astype(BF), joined[:, 2 * GROUP :].astype(BF)

    def project_own(p):
        rows = slice(p * 80, p * 80 + 80)
        q, k, v = project(p, w_ref)
        q_out[rows, :] = q
        kv_out[0, rows, :] = k
        kv_out[1, rows, :] = v

    def project_swap(p):
        q, k, v = project(p, wp)
        rows = slice(p * 80, p * 80 + 80)
        swap_out[0, rows, :] = q
        swap_out[1, rows, :] = k
        swap_out[2, rows, :] = v
        part = pl.ds(p * 80, 80)
        link.send(64 + p, swap_out.at[:, part], swap_in.at[:, part], here.yhi)

    link.wait(0, blocks.at[1], here.zm)
    link.send(2, blocks.at[1], blocks.at[3], here.zp)
    link.wait(1, blocks.at[2], here.zp)
    link.send(3, blocks.at[2], blocks.at[4], here.zm)
    wait_w(27, here.frame_at(1, 0, 0), here.ylo)
    spread(W1, 1)
    modulate(1, 1, 2)
    relay(W0, 0)
    project_own(1)

    link.wait(2, blocks.at[3], here.zm)
    link.send(4, blocks.at[3], blocks.at[5], here.zp)
    link.wait(3, blocks.at[4], here.zp)
    link.send(5, blocks.at[4], blocks.at[6], here.zm)
    relay(W1, 1)
    modulate(2, 3, 4)
    project_own(2)
    finish(W0, 0)

    link.wait(4, blocks.at[5], here.zm)
    link.send(6, blocks.at[5, 0], blocks.at[7, 0], here.zp)
    link.wait(5, blocks.at[6], here.zp)
    link.send(7, blocks.at[6, 1], blocks.at[7, 1], here.zm)
    finish(W1, 1)
    modulate(3, 5, 6)
    project_own(3)
    sib_all(W0, 0)
    sib_all(W1, 1)
    for p in (1, 2, 3):
        project_swap(p)
    link.wait(6, blocks.at[7, 0], here.zm)
    link.wait(7, blocks.at[7, 1], here.zp)
    modulate(0, 0, 7)
    project_swap(0)
    project_own(0)
    wop_out[...] = wop[...]
    for p in (1, 2, 3, 0):
        part = pl.ds(p * 80, 80)
        link.wait(64 + p, swap_in.at[:, part], here.yhi)
    q_out[320:640, :] = swap_in[0]
    kv_out[0, 320:640, :] = swap_in[1]
    kv_out[1, 320:640, :] = swap_in[2]
    link.drain()


def qkv_call(tok, mod, w, wo, qg, kg):
    vm = pl.BlockSpec(memory_space=pltpu.VMEM)
    return pl.pallas_call(
        qkv_kernel,
        out_shape=(
            jax.ShapeDtypeStruct((640, GROUP), BF),
            jax.ShapeDtypeStruct((2, 640, GROUP), BF),
            jax.ShapeDtypeStruct((8, 2, 16, 1536), BF),
            jax.ShapeDtypeStruct((24, 128), F32),
        ),
        in_specs=[vm] * 6,
        out_specs=(vm,) * 4,
        scratch_shapes=[
            pltpu.VMEM((8, 2, 80, 768), BF),
            pltpu.VMEM((16, 16, 64), F32),
            pltpu.VMEM((144, 64), F32),
            pltpu.VMEM((72, 128), F32),
            pltpu.VMEM((3, 16, 192, GROUP), BF),
            pltpu.VMEM((8, 2, 16, 1536), BF),
            pltpu.VMEM((4, 4, 80, 768), BF),
            pltpu.VMEM((3, 320, GROUP), BF),
            pltpu.VMEM((3, 320, GROUP), BF),
            pltpu.SemaphoreType.DMA((68,)),
            pltpu.SemaphoreType.DMA((68,)),
        ],
        compiler_params=pltpu.CompilerParams(
            collective_id=0, has_side_effects=True, vmem_limit_bytes=VMEM_LIMIT
        ),
        name="qkv",
    )(tok, mod, w, wo, qg, kg)


ORDER = [
    (0, 0, 0), (1, 0, 0), (0, 1, 0), (0, 0, 3), (0, 0, 1), (1, 1, 0), (1, 0, 3), (1, 0, 1),
    (0, 1, 3), (0, 1, 1), (0, 0, 2), (1, 1, 3), (1, 1, 1), (1, 0, 2), (0, 1, 2), (1, 1, 2),
]
SLOT = {place: i for i, place in enumerate(ORDER)}
QCOLS = 128


def attend_kernel(q_ref, kv_ref, mixed_out, kbuf, vbuf, qm, vt, acc, top, send_sem, recv_sem):
    here = Place()
    ready = meet([here.sib, here.ylo, here.xp, here.xm])
    link = Link(send_sem, recv_sem)
    kbuf[0] = kv_ref[0]
    vbuf[0] = kv_ref[1].T
    lanes = lax.broadcasted_iota(jnp.int32, (640, GROUP), 1) < HEAD
    zero = jnp.zeros((640, GROUP), BF)
    qm[0:640] = jnp.where(lanes, q_ref[...], zero)
    qm[640:1280] = jnp.where(lanes, zero, q_ref[...])
    acc[...] = jnp.zeros(acc.shape, F32)
    top[...] = jnp.full(top.shape, -1e30, F32)
    ready()

    upper = lax.broadcasted_iota(jnp.int32, (GROUP, 640), 0) < HEAD

    def attend(slot):
        one = jnp.ones((GROUP, 640), BF)
        vt[0] = jnp.where(upper, vbuf[slot], one)
        vt[1] = jnp.where(upper, one, vbuf[slot])

        def mix(cols, head, probs, shrink):
            part = jnp.dot(vt[head], probs, preferred_element_type=F32)
            acc[:, cols] = acc[:, cols] * shrink + part

        for n in range(1280 // QCOLS):
            cols = slice(n * QCOLS, (n + 1) * QCOLS)
            scores = lax.dot_general(
                kbuf[slot], qm[cols, :], (((1,), (1,)), ((), ())), preferred_element_type=F32
            )
            old = top[0:1, cols]
            new = jnp.maximum(old, jnp.max(scores, axis=0, keepdims=True))
            probs = jnp.exp2(scores - new).astype(BF)
            top[0:1, cols] = new
            mix(cols, n * QCOLS // 640, probs, jnp.exp2(old - new))

    def block(kind, place):
        return lambda: (kbuf, vbuf)[kind].at[SLOT[place]]

    def send(src, dst, dev, kinds=(0, 1)):
        for kind in kinds:
            link.send(2 * SLOT[dst] + kind, block(kind, src), block(kind, dst), dev)

    def wait(dst, kinds=(0, 1)):
        for kind in kinds:
            link.wait(2 * SLOT[dst] + kind, block(kind, dst), here.sib)

    def spread(y):
        send((0, y, 0), (0, y, 3), here.xp)
        send((0, y, 0), (0, y, 1), here.xm)
        send((0, y, 0), (1, y, 0), here.sib)

    def relay(y):
        wait((0, y, 3))
        send((0, y, 3), (0, y, 2), here.xp, (0,))
        send((0, y, 3), (1, y, 3), here.sib)
        wait((0, y, 1))
        send((0, y, 1), (0, y, 2), here.xm, (1,))
        send((0, y, 1), (1, y, 1), here.sib)

    def finish(y):
        wait((0, y, 2))
        send((0, y, 2), (1, y, 2), here.sib)

    def arrive_y():
        wait((0, 1, 0))
        spread(1)

    events = {
        0: [lambda: send((0, 0, 0), (0, 1, 0), here.ylo), lambda: spread(0)],
        1: [lambda: wait(ORDER[1])],
        2: [arrive_y, lambda: relay(0)],
        5: [lambda: wait(ORDER[5])],
        6: [lambda: wait(ORDER[6])],
        7: [lambda: wait(ORDER[7])],
        8: [lambda: relay(1)],
        10: [lambda: finish(0)],
        11: [lambda: wait(ORDER[11])],
        12: [lambda: wait(ORDER[12])],
        13: [lambda: wait(ORDER[13])],
        14: [lambda: finish(1)],
        15: [lambda: wait(ORDER[15])],
    }

    def step(t, carry):
        for when, acts in events.items():

            @pl.when(t == when)
            def _():
                for act in acts:
                    act()

        attend(t)
        return carry

    lax.fori_loop(0, 16, step, 0)
    first = acc[0:64, 0:640] / acc[64:65, 0:640]
    second = acc[64:128, 640:1280] / acc[0:1, 640:1280]
    mixed_out[...] = jnp.concatenate([first, second], axis=0).T.astype(BF)
    link.drain()


def attend_call(q, kv):
    vm = pl.BlockSpec(memory_space=pltpu.VMEM)
    return pl.pallas_call(
        attend_kernel,
        out_shape=jax.ShapeDtypeStruct((640, GROUP), BF),
        in_specs=[vm] * 2,
        out_specs=vm,
        scratch_shapes=[
            pltpu.VMEM((16, 640, GROUP), BF),
            pltpu.VMEM((16, GROUP, 640), BF),
            pltpu.VMEM((1280, GROUP), BF),
            pltpu.VMEM((2, GROUP, 640), BF),
            pltpu.VMEM((GROUP, 1280), F32),
            pltpu.VMEM((8, 1280), F32),
            pltpu.SemaphoreType.DMA((32,)),
            pltpu.SemaphoreType.DMA((32,)),
        ],
        compiler_params=pltpu.CompilerParams(
            collective_id=1, has_side_effects=True, vmem_limit_bytes=VMEM_LIMIT
        ),
        name="attend",
    )(q, kv)


def out_kernel(
    mixed_ref, wo_ref, wop_ref, tok_ref, gate_ref, fresh_ref,
    out_ref,
    w2, lhs, other, part, up, down, up_in, down_in, moved, arrived,
    send_sem, recv_sem,
):
    here = Place()
    ready = meet([here.yhi, here.zp, here.zm, here.prev, here.next])
    link = Link(send_sem, recv_sem)
    lhs[:, :GROUP] = mixed_ref[0:320, :]
    ready()
    link.send(0, mixed_ref.at[pl.ds(320, 320)], other, here.yhi)
    w2[0:128, :] = wo_ref[...]
    for h in range(2):
        w2[128:256, h * 1536 : (h + 1) * 1536] = wop_ref[:, h].reshape(128, 1536)
    link.wait(0, other, here.yhi)
    lhs[:, GROUP:] = other[...]

    def multiply(p):
        for h in range(2):
            sums = []
            for k in range(2):
                c = h * 1536 + k * 768
                sums.append(
                    jnp.dot(
                        lhs[p * 80 : p * 80 + 80, :], w2[:, c : c + 768],
                        preferred_element_type=F32,
                    )
                )
            part[0, h] = jnp.concatenate([sums[0][:40], sums[1][:40]], axis=0)
            part[1, h] = jnp.concatenate([sums[0][40:], sums[1][40:]], axis=0)

    multiply(0)
    down[0, 0] = part[1, 0].astype(BF)
    link.send(1, down.at[0, 0], down_in.at[0, 0], here.zm)
    up[0, 1] = part[1, 1].astype(BF)
    link.send(2, up.at[0, 1], up_in.at[0, 1], here.zp)
    own = [part[0, h] for h in range(2)]
    for h in range(2):
        moved[h] = own[h]

    for step, p in ((1, 3), (2, 2), (3, 1)):
        multiply(p)
        for h in ((0, 1) if step > 1 else (1, 0)):
            i = 1 + 4 * step + 2 * h
            if step == 1:
                if h == 0:
                    link.wait(1, down_in.at[0, 0], here.zp)
                else:
                    link.wait(2, up_in.at[0, 1], here.zm)
            else:
                link.wait(i - 4, down_in.at[step - 1, h], here.zp)
                link.wait(i - 3, up_in.at[step - 1, h], here.zm)
            low, high = part[0, h], part[1, h]
            if step > 1 or h == 0:
                low = low + down_in[step - 1, h].astype(F32)
            if step > 1 or h == 1:
                high = high + up_in[step - 1, h].astype(F32)
            down[step, h] = low.astype(BF)
            link.send(i, down.at[step, h], down_in.at[step, h], here.zm)
            up[step, h] = high.astype(BF)
            link.send(i + 1, up.at[step, h], up_in.at[step, h], here.zp)

    tok = to_block(tok_ref[...].astype(F32))
    for h in range(2):
        i = 13 + 2 * h
        link.wait(i, down_in.at[3, h], here.zp)
        link.wait(i + 1, up_in.at[3, h], here.zm)
        total = moved[h] + down_in[3, h].astype(F32) + up_in[3, h].astype(F32)
        pieces = []
        for c in range(6):
            cols = slice(c * 128, (c + 1) * 128)
            t = h * 12 + c
            lo = total[:40, cols] * gate_ref[t : t + 1, :]
            hi = total[40:, cols] * gate_ref[t + 6 : t + 7, :]
            pieces.append(jnp.concatenate([lo, hi], axis=0))
        arrived[0, h] = (tok[h] + jnp.concatenate(pieces, axis=1)).astype(BF)
        link.send(17 + h, arrived.at[0, h], arrived.at[1, h], here.prev)
    last = here.f == 15
    fresh = fresh_ref[...].astype(F32)
    for h in range(2):
        link.wait(17 + h, arrived.at[1, h], here.next)
        got = arrived[1, h].astype(F32)
        for k in range(2):
            cols = slice(h * 1536 + k * 768, h * 1536 + (k + 1) * 768)
            out_ref[:, cols] = jnp.where(last, fresh[:, cols], got[k * 40 : k * 40 + 40]).astype(BF)
    link.drain()


def out_call(mixed, wo, wop, tok, gate, fresh):
    vm = pl.BlockSpec(memory_space=pltpu.VMEM)
    blk = (4, 2, 80, 768)
    return pl.pallas_call(
        out_kernel,
        out_shape=jax.ShapeDtypeStruct((TOK, D), BF),
        in_specs=[vm] * 6,
        out_specs=vm,
        scratch_shapes=[
            pltpu.VMEM((256, D), BF),
            pltpu.VMEM((320, 256), BF),
            pltpu.VMEM((320, GROUP), BF),
            pltpu.VMEM((2, 2, 80, 768), F32),
            pltpu.VMEM(blk, BF),
            pltpu.VMEM(blk, BF),
            pltpu.VMEM(blk, BF),
            pltpu.VMEM(blk, BF),
            pltpu.VMEM((2, 80, 768), F32),
            pltpu.VMEM((2, 2, 80, 768), BF),
            pltpu.SemaphoreType.DMA((19,)),
            pltpu.SemaphoreType.DMA((19,)),
        ],
        compiler_params=pltpu.CompilerParams(
            collective_id=2, has_side_effects=True, vmem_limit_bytes=VMEM_LIMIT
        ),
        name="out",
    )(mixed, wo, wop, tok, gate, fresh)


def body(queue_tokens, timesteps, fresh_noise, w_mod, w_qkv, q_gain, k_gain, w_out):
    tok = queue_tokens[0]
    condition = jax.nn.silu(embed_steps(timesteps)).astype(BF)
    own = jnp.dot(condition, w_mod, preferred_element_type=F32)
    mod = jnp.pad(own.reshape(9, 64), ((0, 7), (0, 0)))
    w = jnp.transpose(w_qkv, (1, 0, 2)).reshape(3, 16, 192, GROUP)
    qg = jnp.concatenate([q_gain, q_gain])[None]
    kg = jnp.concatenate([k_gain, k_gain])[None]
    q, kv, wop, gate = qkv_call(tok, mod, w, w_out, qg, kg)
    mixed = attend_call(q, kv)
    return out_call(mixed, w_out, wop, tok, gate, fresh_noise)[None]


def solution(mesh):
    return jax.shard_map(
        body,
        mesh=mesh,
        in_specs=(
            P("frame", "seq", None),
            P("frame"),
            P("seq", None),
            P(None, "seq"),
            P(None, None, "seq"),
            P(),
            P(),
            P("seq", None),
        ),
        out_specs=P("frame", "seq", None),
        check_vma=False,
    )
```

```python
import math

import jax
import jax.numpy as jnp
from jax import lax
from jax.experimental import pallas as pl
from jax.experimental.pallas import tpu as pltpu
from jax.sharding import PartitionSpec as P

TEMB = 512
TOK = 40
D = 3072
GROUP = 128
HEAD = 64
BF = jnp.bfloat16
F32 = jnp.float32
MESH = pl.DeviceIdType.MESH
VMEM_LIMIT = 56 * 1024 * 1024


def embed_steps(levels):
    halfway = TEMB // 2
    frequency = jnp.exp(-math.log(10000.0) * jnp.arange(halfway, dtype=F32) / halfway)
    angles = levels.astype(F32)[:, None] * frequency[None, :]
    return jnp.concatenate([jnp.cos(angles), jnp.sin(angles)], axis=-1)


class Place:
    def __init__(self):
        f = lax.axis_index("frame")
        s = lax.axis_index("seq")
        self.f, self.s = f, s
        ylo, x, core = f // 8, (f // 2) % 4, f % 2
        yhi, z = s // 8, s % 8
        self.core, self.z, self.yhi_at = core, z, yhi
        self.zs = {d: (z + d + 8) % 8 for d in range(-4, 5)}
        self.coords = (ylo, x, core)
        self.sib = (self.frame_at(0, 0, 1), s)
        self.ylo = (self.frame_at(1, 0, 0), s)
        self.xp = (self.frame_at(0, 1, 0), s)
        self.xm = (self.frame_at(0, 3, 0), s)
        self.zp = self.along_z(1)
        self.zm = self.along_z(-1)
        self.yhi = (f, (1 - yhi) * 8 + z)
        self.prev = ((f + 15) % 16, s)
        self.next = ((f + 1) % 16, s)
        self.far = ((f + 15 + 2 * core) % 16, s)

    def frame_at(self, dy, dx, dc):
        ylo, x, core = self.coords
        return (ylo + dy) % 2 * 8 + (x + dx) % 4 * 2 + (core + dc) % 2

    def z_at(self, d):
        return self.zs[d]

    def along_z(self, d):
        return (self.f, self.yhi_at * 8 + self.z_at(d))


class Link:
    def __init__(self, send_sem, recv_sem):
        self.send_sem, self.recv_sem = send_sem, recv_sem
        self.ids = {}
        self.sent = []

    def _copy(self, name, src, dst, dev):
        i = self.ids.setdefault(name, len(self.ids))
        return pltpu.make_async_remote_copy(
            src_ref=src(),
            dst_ref=dst(),
            send_sem=self.send_sem.at[i],
            recv_sem=self.recv_sem.at[i],
            device_id=dev,
            device_id_type=MESH,
        )

    def send(self, name, src, dst, dev):
        self._copy(name, src, dst, dev).start()
        self.sent.append((name, src, dst, dev))

    def wait(self, name, dst, dev):
        self._copy(name, dst, dst, dev).wait_recv()

    def drain(self):
        for sent in self.sent:
            self._copy(*sent).wait_send()


def meet(devices):
    barrier = pltpu.get_barrier_semaphore()
    for dev in devices:
        pl.semaphore_signal(barrier, inc=1, device_id=dev, device_id_type=MESH)
    return lambda: pl.semaphore_wait(barrier, len(devices))


def to_block(rows):
    pieces = []
    for h in range(2):
        lo = rows[:, h * 1536 : h * 1536 + 768]
        hi = rows[:, h * 1536 + 768 : (h + 1) * 1536]
        pieces.append(jnp.concatenate([lo, hi], axis=0))
    return pieces


def head_norm_pair(x, gain, first):
    a = jnp.sum(jnp.where(first, x, 0.0), axis=-1, keepdims=True) * (1.0 / HEAD)
    b = jnp.sum(jnp.where(first, 0.0, x), axis=-1, keepdims=True) * (1.0 / HEAD)
    c = x - jnp.where(first, a, b)
    sq = c * c
    va = jnp.sum(jnp.where(first, sq, 0.0), axis=-1, keepdims=True) * (1.0 / HEAD)
    vb = jnp.sum(jnp.where(first, 0.0, sq), axis=-1, keepdims=True) * (1.0 / HEAD)
    return c * lax.rsqrt(jnp.where(first, va, vb) + 1e-06) * gain


N_COPIES = 176


def layer_kernel(
    tok_ref, mod_ref, w_ref, wo_ref, qg_ref, kg_ref, fresh_ref,
    out_ref,
    blocks, modbuf, modt, wp, x_scr, swap, qin, kv, qm, vt, acc, top,
    wz, mixed, outbox, lhs, own_part, give, take_in, moved, arrived,
    send_sem, recv_sem,
):
    here = Place()
    f, s, z, core = here.f, here.s, here.z, here.core
    seq_peers = [(f, lax.rem(s + d, 16)) for d in range(1, 16)]
    ready = meet(seq_peers + [here.sib, here.ylo, here.xp, here.xm, here.far])
    link = Link(send_sem, recv_sem)

    tok = tok_ref[...].astype(F32)
    for h, piece in enumerate(to_block(tok)):
        blocks[0, h] = piece.astype(BF)
    modbuf[s] = mod_ref[...]
    for c in range(2):
        for h in range(2):
            wz[z, c, h] = wo_ref[c * 64 : (c + 1) * 64, h * 1536 : (h + 1) * 1536]
    acc[...] = jnp.zeros(acc.shape, F32)
    top[...] = jnp.full(top.shape, -1e30, F32)
    ready()

    for d, dev in enumerate(seq_peers):
        link.send(("mod", d + 1), lambda: modbuf.at[s], lambda: modbuf.at[s], dev)

    def send_tok(j):
        src = (0, 1, 3)[j], (0, 2, 4)[j]
        dst = (1, 3, 5)[j], (2, 4, 6)[j]
        link.send(("up", j), lambda: blocks.at[src[0]], lambda: blocks.at[dst[0]], here.zp)
        link.send(("down", j), lambda: blocks.at[src[1]], lambda: blocks.at[dst[1]], here.zm)

    def wait_tok(j):
        dst = (1, 3, 5)[j], (2, 4, 6)[j]
        link.wait(("up", j), lambda: blocks.at[dst[0]], here.zm)
        link.wait(("down", j), lambda: blocks.at[dst[1]], here.zp)

    send_tok(0)
    link.send("w", lambda: w_ref.at[:, f], lambda: wp.at[:, f], here.yhi)

    def slice_of(who, half=None):
        if half is None:
            return lambda: wp.at[:, who]
        return lambda: wp.at[:, who, pl.ds(96 * half, 96)]

    def w_send(name, who, dev, half=None):
        link.send(("w", name), slice_of(who, half), slice_of(who, half), dev)

    def w_wait(name, who, half=None):
        link.wait(("w", name), slice_of(who, half), here.sib)

    def w_spread(y):
        who = here.frame_at(y, 0, 0)
        w_send((y, "xp"), who, here.xp)
        w_send((y, "xm"), who, here.xm)
        w_send((y, "s0"), who, here.sib)

    def w_relay(y):
        left, right = here.frame_at(y, 3, 0), here.frame_at(y, 1, 0)
        w_wait((y, "xp"), left)
        w_send((y, "xp2"), left, here.xp, 0)
        w_send((y, "s3"), left, here.sib)
        w_wait((y, "xm"), right)
        w_send((y, "xm2"), right, here.xm, 1)
        w_send((y, "s1"), right, here.sib)

    def w_finish(y):
        far = here.frame_at(y, 2, 0)
        w_wait((y, "xp2"), far, 0)
        w_wait((y, "xm2"), far, 1)
        w_send((y, "s2"), far, here.sib)

    def w_from_sib(y):
        for dx in range(4):
            w_wait((y, f"s{dx}"), here.frame_at(y, dx, 1))

    def wo_at(zz, c, h):
        return lambda: wz.at[zz, c, h]

    def wo_start():
        rows = pl.ds(pl.multiple_of(core * 64, 64), 64)
        for h in range(2):
            src = lambda h=h: wo_ref.at[rows, pl.ds(h * 1536, 1536)]
            link.send(("wo", "up", 1, h), src, wo_at(z, core, h), here.zp)
            link.send(("wo", "down", 1, h), src, wo_at(z, core, h), here.zm)

    def wo_relay(d, h):
        for way, zz, dev, last in (("up", here.z_at(-d), here.zp, 0), ("down", here.z_at(d), here.zm, 1)):
            if d == 4 and h != last:
                continue
            at = wo_at(zz, core, h)
            link.wait(("wo", way, d, h), at, dev)
            if d < 3 or (d == 3 and h == last):
                link.send(("wo", way, d + 1, h), at, at, dev)
            link.send(("wo", "sib", way, d, h), at, at, here.sib)

    def wo_from_sib(d, h):
        for way, zz, last in (("up", here.z_at(-d), 0), ("down", here.z_at(d), 1)):
            if d == 4 and h != last:
                continue
            link.wait(("wo", "sib", way, d, h), wo_at(zz, 1 - core, h), here.sib)

    first = lax.broadcasted_iota(jnp.int32, (1, GROUP), 1) < HEAD
    q_scale = math.log2(math.e) / math.sqrt(HEAD)

    def normalise(raw):
        def tile(h, c):
            return raw[h, :, c * 128 : (c + 1) * 128].astype(F32)

        spots = [(h, c) for h in range(2) for c in range(6)]
        total = jnp.zeros((80, 128), F32)
        for h, c in spots:
            total = total + tile(h, c)
        mean = jnp.sum(total[:40] + total[40:], axis=-1, keepdims=True) * (1.0 / D)
        mean = jnp.concatenate([mean, mean], axis=0)
        total = jnp.zeros((80, 128), F32)
        for h, c in spots:
            diff = tile(h, c) - mean
            total = total + diff * diff
        var = jnp.sum(total[:40] + total[40:], axis=-1, keepdims=True) * (1.0 / D)
        inv = lax.rsqrt(var + 1e-05)
        inv = jnp.concatenate([inv, inv], axis=0)
        return lambda h, c: (tile(h, c) - mean) * inv

    def modulate(p, a, b):
        na, nb = normalise(blocks.at[a]), normalise(blocks.at[b])
        for h in range(2):
            for c in range(6):
                va, vb = na(h, c), nb(h, c)
                for half in range(2):
                    t = h * 12 + half * 6 + c
                    rows = slice(half * 40, half * 40 + 40)
                    both = jnp.concatenate([va[rows], vb[rows]], axis=0)
                    scale = 1.0 + modt[24 + t : 25 + t, :]
                    out = both * scale + modt[t : t + 1, :]
                    x_scr[p, t // 6, :, (t % 6) * 128 : (t % 6 + 1) * 128] = out.astype(BF)

    def project(p, n, weights):
        def step(k, total):
            part = jnp.concatenate(
                [weights[j, pl.ds(k * 4, 4)].reshape(768, GROUP) for j in range(3)], axis=1
            )
            rows = x_scr[p : p + n, k].reshape(n * 80, 768)
            return total + jnp.dot(rows, part, preferred_element_type=F32)

        joined = lax.fori_loop(0, 4, step, jnp.zeros((n * 80, 3 * GROUP), F32))
        q = head_norm_pair(joined[:, :GROUP], qg_ref[...], first) * q_scale
        k = head_norm_pair(joined[:, GROUP : 2 * GROUP], kg_ref[...], first)
        return q.astype(BF), k.astype(BF), joined[:, 2 * GROUP :].astype(BF)

    def put_q(p, half, q):
        row = p * 160 + half * 80
        none = jnp.zeros(q.shape, BF)
        qm[row : row + 80, :] = jnp.where(first, q, none)
        qm[640 + row : 720 + row, :] = jnp.where(first, none, q)

    def project_own(p):
        q, k, v = project(p, 1, w_ref)
        put_q(p, 0, q)
        kv[p, 0, 0, 0, 0:80] = k
        kv[p, 0, 0, 1, 0:80] = v

    def project_swap(p, n=1):
        q, k, v = project(p, n, wp)
        for i in range(n):
            rows = slice(i * 80, i * 80 + 80)
            swap[p + i, 0] = q[rows]
            swap[p + i, 1] = k[rows]
            swap[p + i, 2] = v[rows]
        for i in range(n):
            at = p + i
            link.send(
                ("kvswap", at),
                lambda at=at: swap.at[at, pl.ds(1, 2)],
                lambda at=at: kv.at[at, 0, 0, :, pl.ds(80, 80)],
                here.yhi,
            )
            link.send(("qswap", at), lambda at=at: swap.at[at, 0], lambda at=at: qin.at[at], here.yhi)

    def kv_from_y(p):
        link.wait(("kvswap", p), lambda: kv.at[p, 0, 0, :, pl.ds(80, 80)], here.yhi)

    def kv_at(p, x, j, kind=None):
        if kind is None:
            return lambda: kv.at[p, x, j]
        return lambda: kv.at[p, x, j, kind]

    def kv_send(p, src, dst, dev, kind=None):
        link.send(("kv", p, dst, kind), kv_at(p, *src, kind), kv_at(p, *dst, kind), dev)

    def kv_wait(p, dst, kind=None):
        link.wait(("kv", p, dst, kind), kv_at(p, *dst, kind), here.sib)

    def spread(p, y):
        kv_send(p, (0, y), (1, y), here.xp)
        kv_send(p, (0, y), (2, y), here.xm)
        kv_send(p, (0, y), (0, 2 + y), here.sib)

    def begin(p):
        kv_from_y(p)
        kv_send(p, (0, 0), (0, 1), here.ylo)
        spread(p, 0)

    def arrive_y(p):
        kv_wait(p, (0, 1))
        spread(p, 1)

    def relay(p, y):
        kv_wait(p, (1, y))
        kv_send(p, (1, y), (3, y), here.xp, 0)
        kv_send(p, (1, y), (1, 2 + y), here.sib)
        kv_wait(p, (2, y))
        kv_send(p, (2, y), (3, y), here.xm, 1)
        kv_send(p, (2, y), (2, 2 + y), here.sib)

    def finish(p, y):
        kv_wait(p, (3, y), 0)
        kv_wait(p, (3, y), 1)
        kv_send(p, (3, y), (3, 2 + y), here.sib)

    def from_sib(p, x):
        kv_wait(p, (x, 2))
        kv_wait(p, (x, 3))

    w_wait0 = lambda: wp.at[:, f]
    link.wait("w", w_wait0, here.yhi)
    w_send("ylo", f, here.ylo)
    w_spread(0)

    wait_tok(0)
    send_tok(1)
    for d in range(1, 16):
        peer = lax.rem(s + 16 - d, 16)
        link.wait(("mod", d), lambda: modbuf.at[peer], (f, peer))
    for i in range(8):
        low, high = modbuf[2 * i], modbuf[2 * i + 1]
        modt[9 * i : 9 * i + 4, :] = low[0:4]
        modt[9 * i + 4 : 9 * i + 5, :] = low[4:5] + high[0:1]
        modt[9 * i + 5 : 9 * i + 9, :] = high[1:5]
    modulate(1, 1, 2)
    w_wait("ylo", here.frame_at(1, 0, 0))
    w_spread(1)
    w_relay(0)
    project_own(1)

    wait_tok(1)
    send_tok(2)
    w_relay(1)
    modulate(2, 3, 4)
    w_finish(0)
    project_own(2)
    w_finish(1)

    wait_tok(2)
    link.send(("up", 3), lambda: blocks.at[5, 0], lambda: blocks.at[7, 0], here.zp)
    link.send(("down", 3), lambda: blocks.at[6, 1], lambda: blocks.at[7, 1], here.zm)
    wo_start()
    w_from_sib(0)
    w_from_sib(1)
    project_swap(1, 2)
    modulate(3, 5, 6)
    project_own(3)
    begin(1)
    project_swap(3)
    begin(2)
    link.wait(("up", 3), lambda: blocks.at[7, 0], here.zm)
    link.wait(("down", 3), lambda: blocks.at[7, 1], here.zp)
    modulate(0, 0, 7)
    project_swap(0)
    arrive_y(1)
    project_own(0)
    begin(3)
    relay(1, 0)
    arrive_y(2)
    begin(0)
    relay(1, 1)
    relay(2, 0)
    for p in range(4):
        link.wait(("qswap", p), lambda: qin.at[p], here.yhi)
        put_q(p, 1, qin[p])

    upper = lax.broadcasted_iota(jnp.int32, (GROUP, 640), 0) < HEAD

    def attend(t):
        p, x = (t // 4 + 1) % 4, t % 4
        keys = kv[p, x, :, 0].reshape(640, GROUP)
        values = kv[p, x, :, 1].reshape(640, GROUP).T
        one = jnp.ones((GROUP, 640), BF)
        vt[0] = jnp.where(upper, values, one)
        vt[1] = jnp.where(upper, one, values)
        for n in range(10):
            cols = slice(n * 128, (n + 1) * 128)
            scores = lax.dot_general(
                keys, qm[cols, :], (((1,), (1,)), ((), ())), preferred_element_type=F32
            )
            old = top[0:1, cols]
            new = jnp.maximum(old, jnp.max(scores, axis=0, keepdims=True))
            probs = jnp.exp2(scores - new).astype(BF)
            top[0:1, cols] = new
            part = jnp.dot(vt[n // 5], probs, preferred_element_type=F32)
            acc[:, cols] = acc[:, cols] * jnp.exp2(old - new) + part

    events = {
        0: [(arrive_y, 3), (finish, 1, 0)],
        1: [(relay, 2, 1), (finish, 1, 1), (wo_relay, 1, 0)],
        2: [(relay, 3, 0)],
        3: [(arrive_y, 0), (finish, 2, 0), (wo_relay, 1, 1)],
        4: [(finish, 2, 1), (relay, 3, 1)],
        5: [(relay, 0, 0)],
        6: [(finish, 3, 0), (wo_relay, 2, 0)],
        7: [(relay, 0, 1), (finish, 3, 1)],
        8: [(finish, 0, 0)],
        9: [(finish, 0, 1), (wo_relay, 2, 1)],
        11: [(wo_relay, 3, 0)],
        14: [(wo_relay, 3, 1)],
    }
    for t in range(16):
        events.setdefault(t, []).append((from_sib, (t // 4 + 1) % 4, t % 4))

    def step(t, carry):
        for when, acts in events.items():

            @pl.when(t == when)
            def _():
                for act, *args in acts:
                    act(*args)

        attend(t)
        return carry

    lax.fori_loop(0, 16, step, 0)

    upper_part = acc[0:64, 0:640] / acc[64:65, 0:640]
    lower_part = acc[64:128, 640:1280] / acc[0:1, 640:1280]
    mixed[...] = jnp.concatenate([upper_part, lower_part], axis=0).T

    def rows_of(p, b):
        base = p * 160 + b * 40
        return jnp.concatenate([mixed[base : base + 40], mixed[base + 80 : base + 120]], axis=0).astype(BF)

    targets = [(p, b) for p in (1, 2, 3) for b in (0, 1)] + [(0, 1)]
    for i, (p, b) in enumerate(targets):
        outbox[i] = rows_of(p, b)
        dev = here.along_z((4 if p == 0 else p) if b else -p)
        link.send(("mix", i), lambda i=i: outbox.at[i], lambda: lhs.at[z], dev)
    lhs[z] = rows_of(0, 0)
    wo_relay(4, 0)
    wo_relay(4, 1)
    for d in (1, 2, 3, 4):
        for h in range(2):
            wo_from_sib(d, h)
    for i, (p, b) in enumerate(targets):
        source = here.z_at((-4 if p == 0 else -p) if b else p)
        link.wait(("mix", i), lambda source=source: lhs.at[source], here.zp)

    for m in range(4):
        h, c = m // 2, (m % 2) * 768
        total = jnp.zeros((80, 768), F32)
        for i in range(4):
            left = jnp.concatenate([lhs[2 * i], lhs[2 * i + 1]], axis=1)
            right = wz[2 * i : 2 * i + 2, :, h, :, c : c + 768].reshape(256, 768)
            total = total + jnp.dot(left, right, preferred_element_type=F32)
        own_part[m] = total[:40]
        give[m] = jnp.concatenate([total[40:, :384], total[40:, 384:]], axis=0).astype(BF)
        link.send(("give", m), lambda m=m: give.at[m], lambda m=m: take_in.at[m], here.yhi)
    for m in range(4):
        link.wait(("give", m), lambda m=m: take_in.at[m], here.yhi)
        got = take_in[m].astype(F32)
        for half in range(2):
            for c in range(3):
                t = m * 6 + half * 3 + c
                cols = slice(c * 128, (c + 1) * 128)
                total = own_part[m, :, half * 384 + c * 128 : half * 384 + (c + 1) * 128]
                total = total + got[half * 40 : half * 40 + 40, cols]
                base = tok_ref[:, t * 128 : (t + 1) * 128].astype(F32)
                moved[half * 40 : half * 40 + 40, cols] = base + total * modt[48 + t : 49 + t, :]
        arrived[0, m] = moved[...].astype(BF)
        link.send(("shift", m), lambda m=m: arrived.at[0, m], lambda m=m: arrived.at[1, m], here.prev)
    last = f == 15
    fresh = fresh_ref[...].astype(F32)
    for m in range(4):
        link.wait(("shift", m), lambda m=m: arrived.at[1, m], here.next)
        got = arrived[1, m].astype(F32)
        for half in range(2):
            cols = slice(m * 768 + half * 384, m * 768 + (half + 1) * 384)
            out_ref[:, cols] = jnp.where(last, fresh[:, cols], got[half * 40 : half * 40 + 40]).astype(BF)
    link.drain()
    assert len(link.ids) <= N_COPIES, len(link.ids)


def layer_call(*operands):
    vm = pl.BlockSpec(memory_space=pltpu.VMEM)
    return pl.pallas_call(
        layer_kernel,
        out_shape=jax.ShapeDtypeStruct((TOK, D), BF),
        in_specs=[vm] * len(operands),
        out_specs=vm,
        scratch_shapes=[
            pltpu.VMEM((8, 2, 80, 768), BF),
            pltpu.VMEM((16, 8, 128), F32),
            pltpu.VMEM((72, 128), F32),
            pltpu.VMEM((3, 16, 192, GROUP), BF),
            pltpu.VMEM((4, 4, 80, 768), BF),
            pltpu.VMEM((4, 3, 80, GROUP), BF),
            pltpu.VMEM((4, 80, GROUP), BF),
            pltpu.VMEM((4, 4, 4, 2, 160, GROUP), BF),
            pltpu.VMEM((1280, GROUP), BF),
            pltpu.VMEM((2, GROUP, 640), BF),
            pltpu.VMEM((GROUP, 1280), F32),
            pltpu.VMEM((8, 1280), F32),
            pltpu.VMEM((8, 2, 2, 64, 1536), BF),
            pltpu.VMEM((640, GROUP), F32),
            pltpu.VMEM((7, 80, GROUP), BF),
            pltpu.VMEM((8, 80, GROUP), BF),
            pltpu.VMEM((4, 40, 768), F32),
            pltpu.VMEM((4, 80, 384), BF),
            pltpu.VMEM((4, 80, 384), BF),
            pltpu.VMEM((80, 384), F32),
            pltpu.VMEM((2, 4, 80, 384), BF),
            pltpu.SemaphoreType.DMA((N_COPIES,)),
            pltpu.SemaphoreType.DMA((N_COPIES,)),
        ],
        compiler_params=pltpu.CompilerParams(
            collective_id=0, has_side_effects=True, vmem_limit_bytes=VMEM_LIMIT
        ),
        name="layer",
    )(*operands)


def body(queue_tokens, timesteps, fresh_noise, w_mod, w_qkv, q_gain, k_gain, w_out):
    condition = jax.nn.silu(embed_steps(timesteps)).astype(BF)
    own = jnp.dot(condition, w_mod, preferred_element_type=F32)
    even = lax.axis_index("seq") % 2 == 0
    mod = jnp.where(even, jnp.pad(own, ((0, 0), (0, 64))), jnp.pad(own, ((0, 0), (64, 0))))
    mod = jnp.pad(mod.reshape(5, 128), ((0, 3), (0, 0)))
    w = jnp.transpose(w_qkv, (1, 0, 2)).reshape(3, 16, 192, GROUP)
    qg = jnp.concatenate([q_gain, q_gain])[None]
    kg = jnp.concatenate([k_gain, k_gain])[None]
    return layer_call(queue_tokens[0], mod, w, w_out, qg, kg, fresh_noise)[None]


def solution(mesh):
    return jax.shard_map(
        body,
        mesh=mesh,
        in_specs=(
            P("frame", "seq", None),
            P("frame"),
            P("seq", None),
            P(None, "seq"),
            P(None, None, "seq"),
            P(),
            P(),
            P("seq", None),
        ),
        out_specs=P("frame", "seq", None),
        check_vma=False,
    )
```

```python
import math

import jax
import jax.numpy as jnp
from jax import lax
from jax.experimental import pallas as pl
from jax.experimental.pallas import tpu as pltpu
from jax.sharding import PartitionSpec as P

TEMB = 512
TOK = 40
D = 3072
GROUP = 128
HEAD = 64
BF = jnp.bfloat16
F32 = jnp.float32
MESH = pl.DeviceIdType.MESH
VMEM_LIMIT = 56 * 1024 * 1024


def embed_steps(levels):
    halfway = TEMB // 2
    frequency = jnp.exp(-math.log(10000.0) * jnp.arange(halfway, dtype=F32) / halfway)
    angles = levels.astype(F32)[:, None] * frequency[None, :]
    return jnp.concatenate([jnp.cos(angles), jnp.sin(angles)], axis=-1)


class Place:
    def __init__(self):
        f = lax.axis_index("frame")
        s = lax.axis_index("seq")
        self.f, self.s = f, s
        ylo, x, core = f // 8, (f // 2) % 4, f % 2
        yhi, z = s // 8, s % 8
        self.core, self.z, self.yhi_at = core, z, yhi
        self.zs = {d: (z + d + 8) % 8 for d in range(-4, 5)}
        self.coords = (ylo, x, core)
        self.sib = (self.frame_at(0, 0, 1), s)
        self.ylo = (self.frame_at(1, 0, 0), s)
        self.xp = (self.frame_at(0, 1, 0), s)
        self.xm = (self.frame_at(0, 3, 0), s)
        self.zp = self.along_z(1)
        self.zm = self.along_z(-1)
        self.yhi = (f, (1 - yhi) * 8 + z)
        self.prev = ((f + 15) % 16, s)
        self.next = ((f + 1) % 16, s)
        self.far = ((f + 15 + 2 * core) % 16, s)

    def frame_at(self, dy, dx, dc):
        ylo, x, core = self.coords
        return (ylo + dy) % 2 * 8 + (x + dx) % 4 * 2 + (core + dc) % 2

    def z_at(self, d):
        return self.zs[d]

    def along_z(self, d):
        return (self.f, self.yhi_at * 8 + self.z_at(d))


class Link:
    def __init__(self, send_sem, recv_sem):
        self.send_sem, self.recv_sem = send_sem, recv_sem
        self.ids = {}
        self.sent = []

    def _copy(self, name, src, dst, dev):
        i = self.ids.setdefault(name, len(self.ids))
        return pltpu.make_async_remote_copy(
            src_ref=src(),
            dst_ref=dst(),
            send_sem=self.send_sem.at[i],
            recv_sem=self.recv_sem.at[i],
            device_id=dev,
            device_id_type=MESH,
        )

    def send(self, name, src, dst, dev):
        self._copy(name, src, dst, dev).start()
        self.sent.append((name, src, dst, dev))

    def wait(self, name, dst, dev):
        self._copy(name, dst, dst, dev).wait_recv()

    def drain(self):
        for sent in self.sent:
            self._copy(*sent).wait_send()
        self.sent = []


def meet(devices):
    barrier = pltpu.get_barrier_semaphore()
    for dev in devices:
        pl.semaphore_signal(barrier, inc=1, device_id=dev, device_id_type=MESH)
    return lambda: pl.semaphore_wait(barrier, len(devices))


def to_block(rows):
    pieces = []
    for h in range(2):
        lo = rows[:, h * 1536 : h * 1536 + 768]
        hi = rows[:, h * 1536 + 768 : (h + 1) * 1536]
        pieces.append(jnp.concatenate([lo, hi], axis=0))
    return pieces


def head_norm_pair(x, gain, first):
    a = jnp.sum(jnp.where(first, x, 0.0), axis=-1, keepdims=True) * (1.0 / HEAD)
    b = jnp.sum(jnp.where(first, 0.0, x), axis=-1, keepdims=True) * (1.0 / HEAD)
    c = x - jnp.where(first, a, b)
    sq = c * c
    va = jnp.sum(jnp.where(first, sq, 0.0), axis=-1, keepdims=True) * (1.0 / HEAD)
    vb = jnp.sum(jnp.where(first, 0.0, sq), axis=-1, keepdims=True) * (1.0 / HEAD)
    return c * lax.rsqrt(jnp.where(first, va, vb) + 1e-06) * gain


N_COPIES = 176


def layer_kernel(
    tok_ref, cond_ref, wm_hbm, w_hbm, wo_hbm, qg_ref, kg_ref,
    out_ref,
    wm_ref, w_ref, blocks, modbuf, modt, wp, x_scr, swap, qin, kv, qm, vt, acc, top,
    wz, mixed, outbox, lhs, own_part, give, take_in, moved, arrived,
    joined, send_sem, recv_sem, local_sem,
):
    here = Place()
    f, s, z, core = here.f, here.s, here.z, here.core
    seq_peers = [(f, lax.rem(s + d, 16)) for d in range(1, 16)]
    ready = meet(seq_peers + [here.sib, here.ylo, here.xp, here.xm, here.far])
    link = Link(send_sem, recv_sem)

    local = [
        pltpu.make_async_copy(wm_hbm, wm_ref, local_sem.at[0]),
        pltpu.make_async_copy(w_hbm, w_ref, local_sem.at[1]),
    ]
    for c in range(2):
        for h in range(2):
            src = wo_hbm.at[pl.ds(c * 64, 64), pl.ds(h * 1536, 1536)]
            local.append(pltpu.make_async_copy(src, wz.at[z, c, h], local_sem.at[2 + 2 * c + h]))
    for copy in local:
        copy.start()
    tok = tok_ref[...].astype(F32)
    for h, piece in enumerate(to_block(tok)):
        blocks[0, h] = piece.astype(BF)
    local[0].wait()
    own = lax.dot_general(
        jnp.broadcast_to(cond_ref[...].astype(F32), (16, TEMB)).astype(BF), wm_ref[...], (((1,), (1,)), ((), ())), preferred_element_type=F32
    )[0:1]
    gap = jnp.zeros((1, 64), F32)
    even = jnp.concatenate([own, gap], axis=1)
    odd = jnp.concatenate([gap, own], axis=1)
    own = jnp.where(s % 2 == 0, even, odd)
    modbuf[s] = jnp.zeros((8, 128), F32)
    for i in range(5):
        modbuf[s, i : i + 1, :] = own[:, i * 128 : (i + 1) * 128]
    acc[...] = jnp.zeros(acc.shape, F32)
    top[...] = jnp.full(top.shape, -1e30, F32)
    ready()

    link.send("w", lambda: w_hbm.at[:, f], lambda: wp.at[:, f], here.yhi)

    def send_tok(j):
        src = (0, 1, 3)[j], (0, 2, 4)[j]
        dst = (1, 3, 5)[j], (2, 4, 6)[j]
        link.send(("up", j), lambda: blocks.at[src[0]], lambda: blocks.at[dst[0]], here.zp)
        link.send(("down", j), lambda: blocks.at[src[1]], lambda: blocks.at[dst[1]], here.zm)

    def wait_tok(j):
        dst = (1, 3, 5)[j], (2, 4, 6)[j]
        link.wait(("up", j), lambda: blocks.at[dst[0]], here.zm)
        link.wait(("down", j), lambda: blocks.at[dst[1]], here.zp)

    send_tok(0)
    for d, dev in enumerate(seq_peers):
        link.send(("mod", d + 1), lambda: modbuf.at[s], lambda: modbuf.at[s], dev)

    def slice_of(who, half=None):
        if half is None:
            return lambda: wp.at[:, who]
        return lambda: wp.at[:, who, pl.ds(96 * half, 96)]

    def w_send(name, who, dev, half=None):
        link.send(("w", name), slice_of(who, half), slice_of(who, half), dev)

    def w_wait(name, who, half=None):
        link.wait(("w", name), slice_of(who, half), here.sib)

    def w_spread(y):
        who = here.frame_at(y, 0, 0)
        w_send((y, "xp"), who, here.xp)
        w_send((y, "xm"), who, here.xm)
        w_send((y, "s0"), who, here.sib)

    def w_relay(y):
        left, right = here.frame_at(y, 3, 0), here.frame_at(y, 1, 0)
        w_wait((y, "xp"), left)
        w_send((y, "xp2"), left, here.xp, 0)
        w_send((y, "s3"), left, here.sib)
        w_wait((y, "xm"), right)
        w_send((y, "xm2"), right, here.xm, 1)
        w_send((y, "s1"), right, here.sib)

    def w_finish(y):
        far = here.frame_at(y, 2, 0)
        w_wait((y, "xp2"), far, 0)
        w_wait((y, "xm2"), far, 1)
        w_send((y, "s2"), far, here.sib)

    def w_from_sib(y):
        for dx in range(4):
            w_wait((y, f"s{dx}"), here.frame_at(y, dx, 1))

    def wo_at(zz, c, h):
        return lambda: wz.at[zz, c, h]

    def wo_start():
        rows = pl.ds(pl.multiple_of(core * 64, 64), 64)
        for h in range(2):
            src = lambda h=h: wo_hbm.at[rows, pl.ds(h * 1536, 1536)]
            link.send(("wo", "up", 1, h), src, wo_at(z, core, h), here.zp)
            link.send(("wo", "down", 1, h), src, wo_at(z, core, h), here.zm)

    def wo_relay(d, h):
        for way, zz, dev, last in (("up", here.z_at(-d), here.zp, 0), ("down", here.z_at(d), here.zm, 1)):
            if d == 4 and h != last:
                continue
            at = wo_at(zz, core, h)
            link.wait(("wo", way, d, h), at, dev)
            if d < 3 or (d == 3 and h == last):
                link.send(("wo", way, d + 1, h), at, at, dev)
            link.send(("wo", "sib", way, d, h), at, at, here.sib)

    def wo_from_sib(d, h):
        for way, zz, last in (("up", here.z_at(-d), 0), ("down", here.z_at(d), 1)):
            if d == 4 and h != last:
                continue
            link.wait(("wo", "sib", way, d, h), wo_at(zz, 1 - core, h), here.sib)

    first = lax.broadcasted_iota(jnp.int32, (1, GROUP), 1) < HEAD
    q_scale = math.log2(math.e) / math.sqrt(HEAD)

    def normalise(raw):
        def tile(h, c):
            return raw[h, :, c * 128 : (c + 1) * 128].astype(F32)

        spots = [(h, c) for h in range(2) for c in range(6)]
        total = jnp.zeros((80, 128), F32)
        for h, c in spots:
            total = total + tile(h, c)
        mean = jnp.sum(total[:40] + total[40:], axis=-1, keepdims=True) * (1.0 / D)
        mean = jnp.concatenate([mean, mean], axis=0)
        total = jnp.zeros((80, 128), F32)
        for h, c in spots:
            diff = tile(h, c) - mean
            total = total + diff * diff
        var = jnp.sum(total[:40] + total[40:], axis=-1, keepdims=True) * (1.0 / D)
        inv = lax.rsqrt(var + 1e-05)
        inv = jnp.concatenate([inv, inv], axis=0)
        return lambda h, c: (tile(h, c) - mean) * inv

    def modulate(p, a, b):
        na, nb = normalise(blocks.at[a]), normalise(blocks.at[b])
        for h in range(2):
            for c in range(6):
                va, vb = na(h, c), nb(h, c)
                for half in range(2):
                    t = h * 12 + half * 6 + c
                    rows = slice(half * 40, half * 40 + 40)
                    both = jnp.concatenate([va[rows], vb[rows]], axis=0)
                    scale = 1.0 + modt[24 + t : 25 + t, :]
                    out = both * scale + modt[t : t + 1, :]
                    x_scr[p, t // 6, :, (t % 6) * 128 : (t % 6 + 1) * 128] = out.astype(BF)

    q_gain = jnp.concatenate([qg_ref[...]] * 2, axis=1) * q_scale
    k_gain = jnp.concatenate([kg_ref[...]] * 2, axis=1)

    def finish_qkv(qkv):
        q = head_norm_pair(qkv[:, :GROUP], q_gain, first)
        k = head_norm_pair(qkv[:, GROUP : 2 * GROUP], k_gain, first)
        return q.astype(BF), k.astype(BF), qkv[:, 2 * GROUP :].astype(BF)

    def project(p, n=1):
        rows = n * 80
        x = jnp.concatenate([x_scr[p : p + n, k].reshape(rows, 768) for k in range(4)], axis=1)
        sides = [side[j] for side in (wp, w_ref) for j in range(3)]
        for pair in range(3):
            part = jnp.concatenate([sides[2 * pair + i].reshape(D, GROUP) for i in range(2)], axis=1)
            joined[0:rows, pair * 256 : (pair + 1) * 256] = jnp.dot(
                x, part, preferred_element_type=F32
            )
        for i in range(n):
            keep_swap(p + i, *finish_qkv(joined[i * 80 : i * 80 + 80, : 3 * GROUP]))
            send_swap(p + i)
        for i in range(n):
            keep_own(p + i, *finish_qkv(joined[i * 80 : i * 80 + 80, 3 * GROUP :]))

    def put_q(p, half, q):
        row = p * 160 + half * 80
        none = jnp.zeros(q.shape, BF)
        qm[row : row + 80, :] = jnp.where(first, q, none)
        qm[640 + row : 720 + row, :] = jnp.where(first, none, q)

    def keep_own(p, q, k, v):
        put_q(p, 0, q)
        kv[p, 0, 0, 0, 0:80] = k
        kv[p, 0, 0, 1, 0:80] = v

    def keep_swap(p, q, k, v):
        swap[p, 0] = q
        swap[p, 1] = k
        swap[p, 2] = v

    def send_swap(p):
        link.send(
            ("kvswap", p),
            lambda: swap.at[p, pl.ds(1, 2)],
            lambda: kv.at[p, 0, 0, :, pl.ds(80, 80)],
            here.yhi,
        )
        link.send(("qswap", p), lambda: swap.at[p, 0], lambda: qin.at[p], here.yhi)

    def kv_from_y(p):
        link.wait(("kvswap", p), lambda: kv.at[p, 0, 0, :, pl.ds(80, 80)], here.yhi)

    def kv_at(p, x, j, kind=None):
        if kind is None:
            return lambda: kv.at[p, x, j]
        return lambda: kv.at[p, x, j, kind]

    def kv_send(p, src, dst, dev, kind=None):
        link.send(("kv", p, dst, kind), kv_at(p, *src, kind), kv_at(p, *dst, kind), dev)

    def kv_wait(p, dst, kind=None):
        link.wait(("kv", p, dst, kind), kv_at(p, *dst, kind), here.sib)

    def to_sib(p, x):
        src, dst = (lambda: kv.at[p, x, pl.ds(0, 2)]), (lambda: kv.at[p, x, pl.ds(2, 2)])
        link.send(("sib", p, x), src, dst, here.sib)

    def from_sib(p, x):
        link.wait(("sib", p, x), lambda: kv.at[p, x, pl.ds(2, 2)], here.sib)

    def spread(p, y):
        kv_send(p, (0, y), (1, y), here.xp)
        kv_send(p, (0, y), (2, y), here.xm)

    def begin(p):
        kv_from_y(p)
        kv_send(p, (0, 0), (0, 1), here.ylo)
        spread(p, 0)

    def arrive_y(p):
        kv_wait(p, (0, 1))
        spread(p, 1)
        to_sib(p, 0)

    def relay(p, y):
        kv_wait(p, (1, y))
        kv_send(p, (1, y), (3, y), here.xp, 0)
        kv_wait(p, (2, y))
        kv_send(p, (2, y), (3, y), here.xm, 1)
        if y == 1:
            to_sib(p, 1)
            to_sib(p, 2)

    def finish(p):
        for y in range(2):
            kv_wait(p, (3, y), 0)
            kv_wait(p, (3, y), 1)
        to_sib(p, 3)

    w_wait0 = lambda: wp.at[:, f]
    link.wait("w", w_wait0, here.yhi)
    w_send("ylo", f, here.ylo)
    w_spread(0)

    wait_tok(0)
    send_tok(1)
    w_wait("ylo", here.frame_at(1, 0, 0))
    w_spread(1)
    w_relay(0)
    for d in range(1, 16):
        peer = lax.rem(s + 16 - d, 16)
        link.wait(("mod", d), lambda: modbuf.at[peer], (f, peer))
    for i in range(8):
        low, high = modbuf[2 * i], modbuf[2 * i + 1]
        modt[9 * i : 9 * i + 4, :] = low[0:4]
        modt[9 * i + 4 : 9 * i + 5, :] = low[4:5] + high[0:1]
        modt[9 * i + 5 : 9 * i + 9, :] = high[1:5]
    modulate(1, 1, 2)
    w_finish(0)
    local[1].wait()

    wait_tok(1)
    send_tok(2)
    w_relay(1)
    modulate(2, 3, 4)
    w_finish(1)
    w_from_sib(0)
    w_from_sib(1)
    project(1, 2)

    wait_tok(2)
    link.send(("up", 3), lambda: blocks.at[5, 0], lambda: blocks.at[7, 0], here.zp)
    link.send(("down", 3), lambda: blocks.at[6, 1], lambda: blocks.at[7, 1], here.zm)
    begin(1)
    begin(2)
    modulate(3, 5, 6)
    project(3)
    link.wait(("up", 3), lambda: blocks.at[7, 0], here.zm)
    link.wait(("down", 3), lambda: blocks.at[7, 1], here.zp)
    wo_start()
    arrive_y(1)
    modulate(0, 0, 7)
    project(0)
    begin(3)
    for p in (1, 2, 3, 0):
        link.wait(("qswap", p), lambda p=p: qin.at[p], here.yhi)
        put_q(p, 1, qin[p])
    begin(0)

    upper = lax.broadcasted_iota(jnp.int32, (GROUP, 640), 0) < HEAD

    def attend(t):
        p, x = (t // 4 + 1) % 4, t % 4
        keys = kv[p, x, :, 0].reshape(640, GROUP)
        values = kv[p, x, :, 1].reshape(640, GROUP).T
        one = jnp.ones((GROUP, 640), BF)
        vt[0] = jnp.where(upper, values, one)
        vt[1] = jnp.where(upper, one, values)
        for n in range(10):
            cols = slice(n * 128, (n + 1) * 128)
            scores = lax.dot_general(
                keys, qm[cols, :], (((1,), (1,)), ((), ())), preferred_element_type=F32
            )
            old = top[0:1, cols]
            new = jnp.maximum(old, jnp.max(scores, axis=0, keepdims=True))
            probs = jnp.exp2(scores - new).astype(BF)
            top[0:1, cols] = new
            part = jnp.dot(vt[n // 5], probs, preferred_element_type=F32)
            acc[:, cols] = acc[:, cols] * jnp.exp2(old - new) + part

    events = {
        0: [(arrive_y, 2), (relay, 1, 0), (relay, 1, 1), (wo_relay, 1, 0)],
        1: [(relay, 2, 0), (wo_relay, 1, 1)],
        2: [(arrive_y, 3), (finish, 1)],
        3: [(relay, 2, 1)],
        4: [(arrive_y, 0), (relay, 3, 0), (wo_relay, 2, 0)],
        5: [(finish, 2), (relay, 3, 1)],
        6: [(relay, 0, 0), (wo_relay, 2, 1)],
        7: [(relay, 0, 1)],
        8: [(finish, 3)],
        9: [(wo_relay, 3, 0)],
        10: [(finish, 0)],
        12: [(wo_relay, 3, 1)],
        15: [(wo_relay, 4, 0), (wo_relay, 4, 1)],
    }
    for t in range(16):
        events.setdefault(t, []).append((from_sib, (t // 4 + 1) % 4, t % 4))

    def step(t, carry):
        for when, acts in events.items():

            @pl.when(t == when)
            def _():
                for act, *args in acts:
                    act(*args)

        attend(t)
        return carry

    lax.fori_loop(0, 16, step, 0)

    upper_part = acc[0:64, 0:640] / acc[64:65, 0:640]
    lower_part = acc[64:128, 640:1280] / acc[0:1, 640:1280]
    mixed[...] = jnp.concatenate([upper_part, lower_part], axis=0).T

    def rows_of(p, b):
        base = p * 160 + b * 40
        return jnp.concatenate([mixed[base : base + 40], mixed[base + 80 : base + 120]], axis=0).astype(BF)

    targets = [(p, b) for p in (1, 2, 3) for b in (0, 1)] + [(0, 1)]
    for i, (p, b) in enumerate(targets):
        outbox[i] = rows_of(p, b)
        dev = here.along_z((4 if p == 0 else p) if b else -p)
        link.send(("mix", i), lambda i=i: outbox.at[i], lambda: lhs.at[z], dev)
    lhs[z] = rows_of(0, 0)
    link.drain()
    for d in (1, 2, 3, 4):
        for h in range(2):
            wo_from_sib(d, h)
    for i, (p, b) in enumerate(targets):
        source = here.z_at((-4 if p == 0 else -p) if b else p)
        link.wait(("mix", i), lambda source=source: lhs.at[source], here.zp)

    for copy in local[2:]:
        copy.wait()

    left = jnp.concatenate([lhs[i] for i in range(8)], axis=1)
    for m in range(4):
        h, c = m // 2, (m % 2) * 768
        right = wz[:, :, h, :, c : c + 768].reshape(1024, 768)
        total = jnp.dot(left, right, preferred_element_type=F32)
        own_part[m] = total[:40]
        give[m] = jnp.concatenate([total[40:, :384], total[40:, 384:]], axis=0).astype(BF)
        link.send(("give", m), lambda m=m: give.at[m], lambda m=m: take_in.at[m], here.yhi)
    for m in range(4):
        link.wait(("give", m), lambda m=m: take_in.at[m], here.yhi)
        got = take_in[m].astype(F32)
        for half in range(2):
            for c in range(3):
                t = m * 6 + half * 3 + c
                cols = slice(c * 128, (c + 1) * 128)
                total = own_part[m, :, half * 384 + c * 128 : half * 384 + (c + 1) * 128]
                total = total + got[half * 40 : half * 40 + 40, cols]
                base = tok_ref[:, t * 128 : (t + 1) * 128].astype(F32)
                moved[half * 40 : half * 40 + 40, cols] = base + total * modt[48 + t : 49 + t, :]
        arrived[0, m] = moved[...].astype(BF)
        link.send(("shift", m), lambda m=m: arrived.at[0, m], lambda m=m: arrived.at[1, m], here.prev)
    for m in range(4):
        link.wait(("shift", m), lambda m=m: arrived.at[1, m], here.next)
        for half in range(2):
            cols = slice(m * 768 + half * 384, m * 768 + (half + 1) * 384)
            out_ref[:, cols] = arrived[1, m].astype(F32)[half * 40 : half * 40 + 40].astype(BF)
    link.drain()
    assert len(link.ids) <= N_COPIES, len(link.ids)


def layer_call(*operands):
    vm = pl.BlockSpec(memory_space=pltpu.VMEM)
    hbm = pl.BlockSpec(memory_space=pl.ANY)
    return pl.pallas_call(
        layer_kernel,
        out_shape=jax.ShapeDtypeStruct((TOK, D), BF),
        in_specs=[vm, vm, hbm, hbm, hbm, vm, vm],
        out_specs=vm,
        scratch_shapes=[
            pltpu.VMEM((576, TEMB), BF),
            pltpu.VMEM((3, 16, 192, GROUP), BF),
            pltpu.VMEM((8, 2, 80, 768), BF),
            pltpu.VMEM((16, 8, 128), F32),
            pltpu.VMEM((72, 128), F32),
            pltpu.VMEM((3, 16, 192, GROUP), BF),
            pltpu.VMEM((4, 4, 80, 768), BF),
            pltpu.VMEM((4, 3, 80, GROUP), BF),
            pltpu.VMEM((4, 80, GROUP), BF),
            pltpu.VMEM((4, 4, 4, 2, 160, GROUP), BF),
            pltpu.VMEM((1280, GROUP), BF),
            pltpu.VMEM((2, GROUP, 640), BF),
            pltpu.VMEM((GROUP, 1280), F32),
            pltpu.VMEM((8, 1280), F32),
            pltpu.VMEM((8, 2, 2, 64, 1536), BF),
            pltpu.VMEM((640, GROUP), F32),
            pltpu.VMEM((7, 80, GROUP), BF),
            pltpu.VMEM((8, 80, GROUP), BF),
            pltpu.VMEM((4, 40, 768), F32),
            pltpu.VMEM((4, 80, 384), BF),
            pltpu.VMEM((4, 80, 384), BF),
            pltpu.VMEM((80, 384), F32),
            pltpu.VMEM((2, 4, 80, 384), BF),
            pltpu.VMEM((160, 6 * GROUP), F32),
            pltpu.SemaphoreType.DMA((N_COPIES,)),
            pltpu.SemaphoreType.DMA((N_COPIES,)),
            pltpu.SemaphoreType.DMA((6,)),
        ],
        compiler_params=pltpu.CompilerParams(
            collective_id=0, has_side_effects=True, vmem_limit_bytes=VMEM_LIMIT
        ),
        name="layer",
    )(*operands)


def body(queue_tokens, timesteps, fresh_noise, w_mod, w_qkv, q_gain, k_gain, w_out):
    condition = jax.nn.silu(embed_steps(timesteps)).astype(BF)
    w = jnp.transpose(w_qkv, (1, 0, 2)).reshape(3, 16, 192, GROUP)
    arrived = layer_call(queue_tokens[0], condition, w_mod.T, w, w_out, q_gain[None], k_gain[None])
    last = lax.axis_index("frame") == lax.axis_size("frame") - 1
    return jnp.where(last, fresh_noise, arrived)[None]


def solution(mesh):
    return jax.shard_map(
        body,
        mesh=mesh,
        in_specs=(
            P("frame", "seq", None),
            P("frame"),
            P("seq", None),
            P(None, "seq"),
            P(None, None, "seq"),
            P(),
            P(),
            P("seq", None),
        ),
        out_specs=P("frame", "seq", None),
        check_vma=False,
    )
```

```python
import math

import jax
import jax.numpy as jnp
from jax import lax
from jax.experimental import pallas as pl
from jax.experimental.pallas import tpu as pltpu
from jax.sharding import PartitionSpec as P

TEMB = 512
TOK = 40
D = 3072
GROUP = 128
HEAD = 64
BF = jnp.bfloat16
F32 = jnp.float32
MESH = pl.DeviceIdType.MESH
VMEM_LIMIT = 56 * 1024 * 1024


def embed_steps(levels):
    halfway = TEMB // 2
    frequency = jnp.exp(-math.log(10000.0) * jnp.arange(halfway, dtype=F32) / halfway)
    angles = levels.astype(F32)[:, None] * frequency[None, :]
    return jnp.concatenate([jnp.cos(angles), jnp.sin(angles)], axis=-1)


class Place:
    def __init__(self):
        f = lax.axis_index("frame")
        s = lax.axis_index("seq")
        self.f, self.s = f, s
        ylo, x, core = f // 8, (f // 2) % 4, f % 2
        yhi, z = s // 8, s % 8
        self.core, self.z, self.yhi_at = core, z, yhi
        self.zs = {d: (z + d + 8) % 8 for d in range(-4, 5)}
        self.coords = (ylo, x, core)
        self.sib = (self.frame_at(0, 0, 1), s)
        self.ylo = (self.frame_at(1, 0, 0), s)
        self.xp = (self.frame_at(0, 1, 0), s)
        self.xm = (self.frame_at(0, 3, 0), s)
        self.zp = self.along_z(1)
        self.zm = self.along_z(-1)
        self.yhi = (f, (1 - yhi) * 8 + z)
        self.prev = ((f + 15) % 16, s)
        self.next = ((f + 1) % 16, s)
        self.prev_y = ((f + 15) % 16, self.yhi[1])
        self.next_y = ((f + 1) % 16, self.yhi[1])
        self.far = ((f + 15 + 2 * core) % 16, s)

    def frame_at(self, dy, dx, dc):
        ylo, x, core = self.coords
        return (ylo + dy) % 2 * 8 + (x + dx) % 4 * 2 + (core + dc) % 2

    def z_at(self, d):
        return self.zs[d]

    def along_z(self, d):
        return (self.f, self.yhi_at * 8 + self.z_at(d))


class Link:
    def __init__(self, send_sem, recv_sem):
        self.send_sem, self.recv_sem = send_sem, recv_sem
        self.ids = {}
        self.sent = []

    def _copy(self, name, src, dst, dev):
        i = self.ids.setdefault(name, len(self.ids))
        return pltpu.make_async_remote_copy(
            src_ref=src(),
            dst_ref=dst(),
            send_sem=self.send_sem.at[i],
            recv_sem=self.recv_sem.at[i],
            device_id=dev,
            device_id_type=MESH,
        )

    def send(self, name, src, dst, dev):
        self._copy(name, src, dst, dev).start()
        self.sent.append((name, src, dst, dev))

    def wait(self, name, dst, dev):
        self._copy(name, dst, dst, dev).wait_recv()

    def drain(self):
        for sent in self.sent:
            self._copy(*sent).wait_send()
        self.sent = []


def meet(devices):
    barrier = pltpu.get_barrier_semaphore()
    for dev in devices:
        pl.semaphore_signal(barrier, inc=1, device_id=dev, device_id_type=MESH)
    return lambda: pl.semaphore_wait(barrier, len(devices))


def to_block(rows):
    pieces = []
    for h in range(2):
        lo = rows[:, h * 1536 : h * 1536 + 768]
        hi = rows[:, h * 1536 + 768 : (h + 1) * 1536]
        pieces.append(jnp.concatenate([lo, hi], axis=0))
    return pieces


def head_norm_pair(x, gain, first):
    a = jnp.sum(jnp.where(first, x, 0.0), axis=-1, keepdims=True) * (1.0 / HEAD)
    b = jnp.sum(jnp.where(first, 0.0, x), axis=-1, keepdims=True) * (1.0 / HEAD)
    c = x - jnp.where(first, a, b)
    sq = c * c
    va = jnp.sum(jnp.where(first, sq, 0.0), axis=-1, keepdims=True) * (1.0 / HEAD)
    vb = jnp.sum(jnp.where(first, 0.0, sq), axis=-1, keepdims=True) * (1.0 / HEAD)
    return c * lax.rsqrt(jnp.where(first, va, vb) + 1e-06) * gain


N_COPIES = 176


def layer_kernel(
    tok_ref, cond_ref, wm_hbm, w_hbm, wo_hbm, qg_ref, kg_ref,
    out_ref,
    wm_ref, w_ref, blocks, modbuf, modt, wp, x_scr, swap, qin, kv, qm, vt, acc, top,
    wz, mixed, outbox, lhs, give, give_in, keep, keep_in, nexttok, nextgate, s_scr, p_scr,
    joined, send_sem, recv_sem, local_sem,
):
    here = Place()
    f, s, z, core = here.f, here.s, here.z, here.core
    seq_peers = [(f, lax.rem(s + d, 16)) for d in range(1, 16)]
    ready = meet(seq_peers + [here.sib, here.ylo, here.xp, here.xm, here.far, here.prev_y, here.next_y])
    link = Link(send_sem, recv_sem)

    local = [
        pltpu.make_async_copy(wm_hbm, wm_ref, local_sem.at[0]),
        pltpu.make_async_copy(w_hbm, w_ref, local_sem.at[1]),
    ]
    for c in range(2):
        for h in range(2):
            src = wo_hbm.at[pl.ds(c * 64, 64), pl.ds(h * 1536, 1536)]
            local.append(pltpu.make_async_copy(src, wz.at[z, c, h], local_sem.at[2 + 2 * c + h]))
    for copy in local:
        copy.start()
    tok = tok_ref[...].astype(F32)
    for h, piece in enumerate(to_block(tok)):
        blocks[0, h] = piece.astype(BF)
    local[0].wait()
    own = lax.dot_general(
        jnp.broadcast_to(cond_ref[...].astype(F32), (16, TEMB)).astype(BF), wm_ref[...], (((1,), (1,)), ((), ())), preferred_element_type=F32
    )[0:1]
    gap = jnp.zeros((1, 64), F32)
    even = jnp.concatenate([own, gap], axis=1)
    odd = jnp.concatenate([gap, own], axis=1)
    own = jnp.where(s % 2 == 0, even, odd)
    modbuf[s] = jnp.zeros((8, 128), F32)
    for i in range(5):
        modbuf[s, i : i + 1, :] = own[:, i * 128 : (i + 1) * 128]
    acc[...] = jnp.zeros(acc.shape, F32)
    top[...] = jnp.full(top.shape, -1e30, F32)
    ready()

    link.send("w", lambda: w_hbm.at[:, f], lambda: wp.at[:, f], here.yhi)

    def send_tok(j):
        src = (0, 1, 3)[j], (0, 2, 4)[j]
        dst = (1, 3, 5)[j], (2, 4, 6)[j]
        link.send(("up", j), lambda: blocks.at[src[0]], lambda: blocks.at[dst[0]], here.zp)
        link.send(("down", j), lambda: blocks.at[src[1]], lambda: blocks.at[dst[1]], here.zm)

    def wait_tok(j):
        dst = (1, 3, 5)[j], (2, 4, 6)[j]
        link.wait(("up", j), lambda: blocks.at[dst[0]], here.zm)
        link.wait(("down", j), lambda: blocks.at[dst[1]], here.zp)

    send_tok(0)
    for d, dev in enumerate(seq_peers):
        link.send(("mod", d + 1), lambda: modbuf.at[s], lambda: modbuf.at[s], dev)

    def slice_of(who, half=None):
        if half is None:
            return lambda: wp.at[:, who]
        return lambda: wp.at[:, who, pl.ds(96 * half, 96)]

    def w_send(name, who, dev, half=None):
        link.send(("w", name), slice_of(who, half), slice_of(who, half), dev)

    def w_wait(name, who, half=None):
        link.wait(("w", name), slice_of(who, half), here.sib)

    def w_spread(y):
        who = here.frame_at(y, 0, 0)
        w_send((y, "xp"), who, here.xp)
        w_send((y, "xm"), who, here.xm)
        w_send((y, "s0"), who, here.sib)

    def w_relay(y):
        left, right = here.frame_at(y, 3, 0), here.frame_at(y, 1, 0)
        w_wait((y, "xp"), left)
        w_send((y, "xp2"), left, here.xp, 0)
        w_send((y, "s3"), left, here.sib)
        w_wait((y, "xm"), right)
        w_send((y, "xm2"), right, here.xm, 1)
        w_send((y, "s1"), right, here.sib)

    def w_finish(y):
        far = here.frame_at(y, 2, 0)
        w_wait((y, "xp2"), far, 0)
        w_wait((y, "xm2"), far, 1)
        w_send((y, "s2"), far, here.sib)

    def w_from_sib(y):
        for dx in range(4):
            w_wait((y, f"s{dx}"), here.frame_at(y, dx, 1))

    def wo_at(zz, c, h):
        return lambda: wz.at[zz, c, h]

    def wo_start():
        rows = pl.ds(pl.multiple_of(core * 64, 64), 64)
        for h in range(2):
            src = lambda h=h: wo_hbm.at[rows, pl.ds(h * 1536, 1536)]
            link.send(("wo", "up", 1, h), src, wo_at(z, core, h), here.zp)
            link.send(("wo", "down", 1, h), src, wo_at(z, core, h), here.zm)

    def wo_relay(d, h):
        for way, zz, dev, last in (("up", here.z_at(-d), here.zp, 0), ("down", here.z_at(d), here.zm, 1)):
            if d == 4 and h != last:
                continue
            at = wo_at(zz, core, h)
            link.wait(("wo", way, d, h), at, dev)
            if d < 3 or (d == 3 and h == last):
                link.send(("wo", way, d + 1, h), at, at, dev)
            link.send(("wo", "sib", way, d, h), at, at, here.sib)

    def wo_from_sib(d, h):
        for way, zz, last in (("up", here.z_at(-d), 0), ("down", here.z_at(d), 1)):
            if d == 4 and h != last:
                continue
            link.wait(("wo", "sib", way, d, h), wo_at(zz, 1 - core, h), here.sib)

    first = lax.broadcasted_iota(jnp.int32, (1, GROUP), 1) < HEAD
    q_scale = math.log2(math.e) / math.sqrt(HEAD)

    def normalise(raw):
        def tile(h, c):
            return raw[h, :, c * 128 : (c + 1) * 128].astype(F32)

        spots = [(h, c) for h in range(2) for c in range(6)]
        total = jnp.zeros((80, 128), F32)
        for h, c in spots:
            total = total + tile(h, c)
        mean = jnp.sum(total[:40] + total[40:], axis=-1, keepdims=True) * (1.0 / D)
        mean = jnp.concatenate([mean, mean], axis=0)
        total = jnp.zeros((80, 128), F32)
        for h, c in spots:
            diff = tile(h, c) - mean
            total = total + diff * diff
        var = jnp.sum(total[:40] + total[40:], axis=-1, keepdims=True) * (1.0 / D)
        inv = lax.rsqrt(var + 1e-05)
        inv = jnp.concatenate([inv, inv], axis=0)
        return lambda h, c: (tile(h, c) - mean) * inv

    def modulate(p, a, b):
        na, nb = normalise(blocks.at[a]), normalise(blocks.at[b])
        for h in range(2):
            for c in range(6):
                va, vb = na(h, c), nb(h, c)
                for half in range(2):
                    t = h * 12 + half * 6 + c
                    rows = slice(half * 40, half * 40 + 40)
                    both = jnp.concatenate([va[rows], vb[rows]], axis=0)
                    scale = 1.0 + modt[24 + t : 25 + t, :]
                    out = both * scale + modt[t : t + 1, :]
                    x_scr[p, t // 6, :, (t % 6) * 128 : (t % 6 + 1) * 128] = out.astype(BF)

    q_gain = jnp.concatenate([qg_ref[...]] * 2, axis=1) * q_scale
    k_gain = jnp.concatenate([kg_ref[...]] * 2, axis=1)

    def finish_qkv(qkv):
        q = head_norm_pair(qkv[:, :GROUP], q_gain, first)
        k = head_norm_pair(qkv[:, GROUP : 2 * GROUP], k_gain, first)
        return q.astype(BF), k.astype(BF), qkv[:, 2 * GROUP :].astype(BF)

    def project(p, n=1):
        rows = n * 80
        x = jnp.concatenate([x_scr[p : p + n, k].reshape(rows, 768) for k in range(4)], axis=1)
        sides = [side[j] for side in (wp, w_ref) for j in range(3)]
        for pair in range(3):
            part = jnp.concatenate([sides[2 * pair + i].reshape(D, GROUP) for i in range(2)], axis=1)
            joined[0:rows, pair * 256 : (pair + 1) * 256] = jnp.dot(
                x, part, preferred_element_type=F32
            )
        for i in range(n):
            keep_swap(p + i, *finish_qkv(joined[i * 80 : i * 80 + 80, : 3 * GROUP]))
            send_swap(p + i)
        for i in range(n):
            keep_own(p + i, *finish_qkv(joined[i * 80 : i * 80 + 80, 3 * GROUP :]))

    def put_q(p, half, q):
        row = p * 160 + half * 80
        none = jnp.zeros(q.shape, BF)
        qm[row : row + 80, :] = jnp.where(first, q, none)
        qm[640 + row : 720 + row, :] = jnp.where(first, none, q)

    def keep_own(p, q, k, v):
        put_q(p, 0, q)
        kv[p, 0, 0, 0, 0:80] = k
        kv[p, 0, 0, 1, 0:80] = v

    def keep_swap(p, q, k, v):
        swap[p, 0] = q
        swap[p, 1] = k
        swap[p, 2] = v

    def send_swap(p):
        link.send(
            ("kvswap", p),
            lambda: swap.at[p, pl.ds(1, 2)],
            lambda: kv.at[p, 0, 0, :, pl.ds(80, 80)],
            here.yhi,
        )
        link.send(("qswap", p), lambda: swap.at[p, 0], lambda: qin.at[p], here.yhi)

    def kv_from_y(p):
        link.wait(("kvswap", p), lambda: kv.at[p, 0, 0, :, pl.ds(80, 80)], here.yhi)

    def kv_at(p, x, j, kind=None):
        if kind is None:
            return lambda: kv.at[p, x, j]
        return lambda: kv.at[p, x, j, kind]

    def kv_send(p, src, dst, dev, kind=None):
        link.send(("kv", p, dst, kind), kv_at(p, *src, kind), kv_at(p, *dst, kind), dev)

    def kv_wait(p, dst, kind=None):
        link.wait(("kv", p, dst, kind), kv_at(p, *dst, kind), here.sib)

    def to_sib(p, x):
        src, dst = (lambda: kv.at[p, x, pl.ds(0, 2)]), (lambda: kv.at[p, x, pl.ds(2, 2)])
        link.send(("sib", p, x), src, dst, here.sib)

    def from_sib(p, x):
        link.wait(("sib", p, x), lambda: kv.at[p, x, pl.ds(2, 2)], here.sib)

    def spread(p, y):
        kv_send(p, (0, y), (1, y), here.xp)
        kv_send(p, (0, y), (2, y), here.xm)

    def begin(p):
        kv_from_y(p)
        kv_send(p, (0, 0), (0, 1), here.ylo)
        spread(p, 0)

    def arrive_y(p):
        kv_wait(p, (0, 1))
        spread(p, 1)
        to_sib(p, 0)

    def relay(p, y):
        kv_wait(p, (1, y))
        kv_send(p, (1, y), (3, y), here.xp, 0)
        kv_wait(p, (2, y))
        kv_send(p, (2, y), (3, y), here.xm, 1)
        if y == 1:
            to_sib(p, 1)
            to_sib(p, 2)

    def finish(p):
        for y in range(2):
            kv_wait(p, (3, y), 0)
            kv_wait(p, (3, y), 1)
        to_sib(p, 3)

    w_wait0 = lambda: wp.at[:, f]
    link.wait("w", w_wait0, here.yhi)
    w_send("ylo", f, here.ylo)
    w_spread(0)

    wait_tok(0)
    send_tok(1)
    w_wait("ylo", here.frame_at(1, 0, 0))
    w_spread(1)
    w_relay(0)
    for d in range(1, 16):
        peer = lax.rem(s + 16 - d, 16)
        link.wait(("mod", d), lambda: modbuf.at[peer], (f, peer))
    for i in range(8):
        low, high = modbuf[2 * i], modbuf[2 * i + 1]
        modt[9 * i : 9 * i + 4, :] = low[0:4]
        modt[9 * i + 4 : 9 * i + 5, :] = low[4:5] + high[0:1]
        modt[9 * i + 5 : 9 * i + 9, :] = high[1:5]
    modulate(1, 1, 2)
    w_finish(0)
    local[1].wait()

    wait_tok(1)
    send_tok(2)
    w_relay(1)
    modulate(2, 3, 4)
    w_finish(1)
    w_from_sib(0)
    w_from_sib(1)
    project(1, 2)

    wait_tok(2)
    link.send(("up", 3), lambda: blocks.at[5, 0], lambda: blocks.at[7, 0], here.zp)
    link.send(("down", 3), lambda: blocks.at[6, 1], lambda: blocks.at[7, 1], here.zm)
    begin(1)
    begin(2)
    modulate(3, 5, 6)
    project(3)
    link.wait(("up", 3), lambda: blocks.at[7, 0], here.zm)
    link.wait(("down", 3), lambda: blocks.at[7, 1], here.zp)
    wo_start()
    arrive_y(1)
    modulate(0, 0, 7)
    project(0)
    begin(3)
    for p in (1, 2, 3, 0):
        link.wait(("qswap", p), lambda p=p: qin.at[p], here.yhi)
        put_q(p, 1, qin[p])
    begin(0)

    upper = lax.broadcasted_iota(jnp.int32, (GROUP, 640), 0) < HEAD

    def attend(t):
        p, x = (t // 4 + 1) % 4, t % 4
        keys = kv[p, x, :, 0].reshape(640, GROUP)
        values = kv[p, x, :, 1].reshape(640, GROUP).T
        one = jnp.ones((GROUP, 640), BF)
        vt[0] = jnp.where(upper, values, one)
        vt[1] = jnp.where(upper, one, values)
        def score(n):
            s_scr[n % 2] = lax.dot_general(
                keys, qm[n * 128 : (n + 1) * 128, :], (((1,), (1,)), ((), ())),
                preferred_element_type=F32,
            )

        def weigh(n):
            cols = slice(n * 128, (n + 1) * 128)
            old = top[0:1, cols]
            new = jnp.maximum(old, jnp.max(s_scr[n % 2], axis=0, keepdims=True))
            p_scr[n % 2] = jnp.exp2(s_scr[n % 2] - new).astype(BF)
            top[0:1, cols] = new
            return jnp.exp2(old - new)

        def mix(n, shrink):
            cols = slice(n * 128, (n + 1) * 128)
            part = jnp.dot(vt[n // 5], p_scr[n % 2], preferred_element_type=F32)
            acc[:, cols] = acc[:, cols] * shrink + part

        score(0)
        shrink = None
        for n in range(10):
            if n < 9:
                score(n + 1)
            now = weigh(n)
            if n:
                mix(n - 1, shrink)
            shrink = now
        mix(9, shrink)

    def send_base():
        link.send("tok", lambda: blocks.at[0], lambda: nexttok, here.prev)
        link.send("gate", lambda: modt.at[pl.ds(48, 24)], lambda: nextgate, here.prev)

    events = {
        0: [(arrive_y, 2), (relay, 1, 0), (relay, 1, 1), (wo_relay, 1, 0)],
        1: [(relay, 2, 0), (wo_relay, 1, 1)],
        2: [(arrive_y, 3), (finish, 1)],
        3: [(relay, 2, 1)],
        4: [(arrive_y, 0), (relay, 3, 0), (wo_relay, 2, 0)],
        5: [(finish, 2), (relay, 3, 1)],
        6: [(relay, 0, 0), (wo_relay, 2, 1)],
        7: [(relay, 0, 1)],
        8: [(finish, 3)],
        9: [(wo_relay, 3, 0)],
        10: [(finish, 0)],
        12: [(wo_relay, 3, 1)],
        13: [(send_base,)],
        15: [(wo_relay, 4, 0), (wo_relay, 4, 1)],
    }
    for t in range(16):
        events.setdefault(t, []).append((from_sib, (t // 4 + 1) % 4, t % 4))

    def step(t, carry):
        for when, acts in events.items():

            @pl.when(t == when)
            def _():
                for act, *args in acts:
                    act(*args)

        attend(t)
        return carry

    lax.fori_loop(0, 16, step, 0)

    upper_part = acc[0:64, 0:640] / acc[64:65, 0:640]
    lower_part = acc[64:128, 640:1280] / acc[0:1, 640:1280]
    mixed[...] = jnp.concatenate([upper_part, lower_part], axis=0).T

    def rows_of(p, b):
        base = p * 160 + b * 40
        return jnp.concatenate([mixed[base : base + 40], mixed[base + 80 : base + 120]], axis=0).astype(BF)

    targets = [(0, 1)] + [(p, b) for p in (3, 2, 1) for b in (0, 1)]
    for i, (p, b) in enumerate(targets):
        outbox[i] = rows_of(p, b)
        dev = here.along_z((4 if p == 0 else p) if b else -p)
        link.send(("mix", i), lambda i=i: outbox.at[i], lambda: lhs.at[z], dev)
    lhs[z] = rows_of(0, 0)
    link.drain()
    for d in (1, 2, 3, 4):
        for h in range(2):
            wo_from_sib(d, h)
    for i, (p, b) in enumerate(targets):
        source = here.z_at((-4 if p == 0 else -p) if b else p)
        link.wait(("mix", i), lambda source=source: lhs.at[source], here.zp)

    for copy in local[2:]:
        copy.wait()

    left = jnp.concatenate([lhs[i] for i in range(8)], axis=1)
    for m in range(4):
        h, c = m // 2, (m % 2) * 768
        right = wz[:, :, h, :, c : c + 768].reshape(1024, 768)
        total = jnp.dot(left, right, preferred_element_type=F32)
        give[m] = jnp.concatenate([total[40:, :384], total[40:, 384:]], axis=0).astype(BF)
        link.send(("give", m), lambda m=m: give.at[m], lambda m=m: give_in.at[m], here.prev_y)
        keep[m] = jnp.concatenate([total[:40, :384], total[:40, 384:]], axis=0).astype(BF)
        link.send(("keep", m), lambda m=m: keep.at[m], lambda m=m: keep_in.at[m], here.prev)
    link.wait("tok", lambda: nexttok, here.next)
    link.wait("gate", lambda: nextgate, here.next)
    for m in range(4):
        h, k = m // 2, m % 2
        base = nexttok[h].astype(F32)[k * 40 : k * 40 + 40]
        link.wait(("keep", m), lambda m=m: keep_in.at[m], here.next)
        link.wait(("give", m), lambda m=m: give_in.at[m], here.next_y)
        total = keep_in[m].astype(F32) + give_in[m].astype(F32)
        for half in range(2):
            for c in range(3):
                t = m * 6 + half * 3 + c
                term = total[half * 40 : half * 40 + 40, c * 128 : (c + 1) * 128] * nextgate[t : t + 1, :]
                at = half * 384 + c * 128
                out_ref[:, t * 128 : (t + 1) * 128] = (base[:, at : at + 128] + term).astype(BF)
    link.drain()
    assert len(link.ids) <= N_COPIES, len(link.ids)


def layer_call(*operands):
    vm = pl.BlockSpec(memory_space=pltpu.VMEM)
    hbm = pl.BlockSpec(memory_space=pl.ANY)
    return pl.pallas_call(
        layer_kernel,
        out_shape=jax.ShapeDtypeStruct((TOK, D), BF),
        in_specs=[vm, vm, hbm, hbm, hbm, vm, vm],
        out_specs=vm,
        scratch_shapes=[
            pltpu.VMEM((576, TEMB), BF),
            pltpu.VMEM((3, 16, 192, GROUP), BF),
            pltpu.VMEM((8, 2, 80, 768), BF),
            pltpu.VMEM((16, 8, 128), F32),
            pltpu.VMEM((72, 128), F32),
            pltpu.VMEM((3, 16, 192, GROUP), BF),
            pltpu.VMEM((4, 4, 80, 768), BF),
            pltpu.VMEM((4, 3, 80, GROUP), BF),
            pltpu.VMEM((4, 80, GROUP), BF),
            pltpu.VMEM((4, 4, 4, 2, 160, GROUP), BF),
            pltpu.VMEM((1280, GROUP), BF),
            pltpu.VMEM((2, GROUP, 640), BF),
            pltpu.VMEM((GROUP, 1280), F32),
            pltpu.VMEM((8, 1280), F32),
            pltpu.VMEM((8, 2, 2, 64, 1536), BF),
            pltpu.VMEM((640, GROUP), F32),
            pltpu.VMEM((7, 80, GROUP), BF),
            pltpu.VMEM((8, 80, GROUP), BF),
            pltpu.VMEM((4, 80, 384), BF),
            pltpu.VMEM((4, 80, 384), BF),
            pltpu.VMEM((4, 80, 384), BF),
            pltpu.VMEM((4, 80, 384), BF),
            pltpu.VMEM((2, 80, 768), BF),
            pltpu.VMEM((24, 128), F32),
            pltpu.VMEM((2, 640, GROUP), F32),
            pltpu.VMEM((2, 640, GROUP), BF),
            pltpu.VMEM((160, 6 * GROUP), F32),
            pltpu.SemaphoreType.DMA((N_COPIES,)),
            pltpu.SemaphoreType.DMA((N_COPIES,)),
            pltpu.SemaphoreType.DMA((6,)),
        ],
        compiler_params=pltpu.CompilerParams(
            collective_id=0, has_side_effects=True, vmem_limit_bytes=VMEM_LIMIT
        ),
        name="layer",
    )(*operands)


def body(queue_tokens, timesteps, fresh_noise, w_mod, w_qkv, q_gain, k_gain, w_out):
    condition = jax.nn.silu(embed_steps(timesteps)).astype(BF)
    w = jnp.transpose(w_qkv, (1, 0, 2)).reshape(3, 16, 192, GROUP)
    arrived = layer_call(queue_tokens[0], condition, w_mod.T, w, w_out, q_gain[None], k_gain[None])
    last = lax.axis_index("frame") == lax.axis_size("frame") - 1
    return jnp.where(last, fresh_noise, arrived)[None]


def solution(mesh):
    return jax.shard_map(
        body,
        mesh=mesh,
        in_specs=(
            P("frame", "seq", None),
            P("frame"),
            P("seq", None),
            P(None, "seq"),
            P(None, None, "seq"),
            P(),
            P(),
            P("seq", None),
        ),
        out_specs=P("frame", "seq", None),
        check_vma=False,
    )
```

```python
import math

import jax
import jax.numpy as jnp
from jax import lax
from jax.experimental import pallas as pl
from jax.experimental.pallas import tpu as pltpu
from jax.sharding import PartitionSpec as P

TEMB = 512
TOK = 40
D = 3072
GROUP = 128
HEAD = 64
BF = jnp.bfloat16
F32 = jnp.float32
MESH = pl.DeviceIdType.MESH
VMEM_LIMIT = 56 * 1024 * 1024


def embed_steps(levels):
    halfway = TEMB // 2
    frequency = jnp.exp(-math.log(10000.0) * jnp.arange(halfway, dtype=F32) / halfway)
    angles = levels.astype(F32)[:, None] * frequency[None, :]
    return jnp.concatenate([jnp.cos(angles), jnp.sin(angles)], axis=-1)


class Place:
    def __init__(self):
        f = lax.axis_index("frame")
        s = lax.axis_index("seq")
        self.f, self.s = f, s
        ylo, x, core = f // 8, (f // 2) % 4, f % 2
        yhi, z = s // 8, s % 8
        self.core, self.z, self.yhi_at = core, z, yhi
        self.zs = {d: (z + d + 8) % 8 for d in range(-4, 5)}
        self.coords = (ylo, x, core)
        self.sib = (self.frame_at(0, 0, 1), s)
        self.ylo = (self.frame_at(1, 0, 0), s)
        self.xp = (self.frame_at(0, 1, 0), s)
        self.xm = (self.frame_at(0, 3, 0), s)
        self.zp = self.along_z(1)
        self.zm = self.along_z(-1)
        self.yhi = (f, (1 - yhi) * 8 + z)
        self.prev = ((f + 15) % 16, s)
        self.next = ((f + 1) % 16, s)
        self.prev_y = ((f + 15) % 16, self.yhi[1])
        self.next_y = ((f + 1) % 16, self.yhi[1])
        self.far = ((f + 15 + 2 * core) % 16, s)

    def frame_at(self, dy, dx, dc):
        ylo, x, core = self.coords
        return (ylo + dy) % 2 * 8 + (x + dx) % 4 * 2 + (core + dc) % 2

    def z_at(self, d):
        return self.zs[d]

    def along_z(self, d):
        return (self.f, self.yhi_at * 8 + self.z_at(d))


class Link:
    def __init__(self, send_sem, recv_sem):
        self.send_sem, self.recv_sem = send_sem, recv_sem
        self.ids = {}
        self.sent = []

    def _copy(self, name, src, dst, dev):
        i = self.ids.setdefault(name, len(self.ids))
        return pltpu.make_async_remote_copy(
            src_ref=src(),
            dst_ref=dst(),
            send_sem=self.send_sem.at[i],
            recv_sem=self.recv_sem.at[i],
            device_id=dev,
            device_id_type=MESH,
        )

    def send(self, name, src, dst, dev):
        self._copy(name, src, dst, dev).start()
        self.sent.append((name, src, dst, dev))

    def wait(self, name, dst, dev):
        self._copy(name, dst, dst, dev).wait_recv()

    def drain(self):
        for sent in self.sent:
            self._copy(*sent).wait_send()
        self.sent = []


def meet(devices):
    barrier = pltpu.get_barrier_semaphore()
    for dev in devices:
        pl.semaphore_signal(barrier, inc=1, device_id=dev, device_id_type=MESH)
    return lambda: pl.semaphore_wait(barrier, len(devices))


def to_block(rows):
    pieces = []
    for h in range(2):
        lo = rows[:, h * 1536 : h * 1536 + 768]
        hi = rows[:, h * 1536 + 768 : (h + 1) * 1536]
        pieces.append(jnp.concatenate([lo, hi], axis=0))
    return pieces


def head_norm_pair(x, gain, first):
    a = jnp.sum(jnp.where(first, x, 0.0), axis=-1, keepdims=True) * (1.0 / HEAD)
    b = jnp.sum(jnp.where(first, 0.0, x), axis=-1, keepdims=True) * (1.0 / HEAD)
    c = x - jnp.where(first, a, b)
    sq = c * c
    va = jnp.sum(jnp.where(first, sq, 0.0), axis=-1, keepdims=True) * (1.0 / HEAD)
    vb = jnp.sum(jnp.where(first, 0.0, sq), axis=-1, keepdims=True) * (1.0 / HEAD)
    return c * lax.rsqrt(jnp.where(first, va, vb) + 1e-06) * gain


N_COPIES = 200


def layer_kernel(
    tok_ref, cond_ref, wm_hbm, w_hbm, wo_hbm, qg_ref, kg_ref,
    out_ref,
    wm_ref, w_ref, blocks, modbuf, modt, wp, x_scr, swap, qin, kv, qm, vt, acc, top,
    wz, mixed, outbox, lhs, give, give_in, keep, keep_in, nexttok, nextgate, s_scr, p_scr,
    joined, send_sem, recv_sem, local_sem,
):
    here = Place()
    f, s, z, core = here.f, here.s, here.z, here.core
    seq_peers = [(f, lax.rem(s + d, 16)) for d in range(1, 16)]
    ready = meet(seq_peers + [here.sib, here.ylo, here.xp, here.xm, here.far, here.prev_y, here.next_y])
    link = Link(send_sem, recv_sem)

    local = [
        pltpu.make_async_copy(wm_hbm, wm_ref, local_sem.at[0]),
        pltpu.make_async_copy(w_hbm, w_ref, local_sem.at[1]),
    ]
    for c in range(2):
        for h in range(2):
            src = wo_hbm.at[pl.ds(c * 64, 64), pl.ds(h * 1536, 1536)]
            local.append(pltpu.make_async_copy(src, wz.at[z, c, h], local_sem.at[2 + 2 * c + h]))
    for copy in local:
        copy.start()
    tok = tok_ref[...].astype(F32)
    for h, piece in enumerate(to_block(tok)):
        blocks[0, h] = piece.astype(BF)
    local[0].wait()
    own = lax.dot_general(
        jnp.broadcast_to(cond_ref[...].astype(F32), (16, TEMB)).astype(BF), wm_ref[...], (((1,), (1,)), ((), ())), preferred_element_type=F32
    )[0:1]
    gap = jnp.zeros((1, 64), F32)
    even = jnp.concatenate([own, gap], axis=1)
    odd = jnp.concatenate([gap, own], axis=1)
    own = jnp.where(s % 2 == 0, even, odd)
    modbuf[s] = jnp.zeros((8, 128), F32)
    for i in range(5):
        modbuf[s, i : i + 1, :] = own[:, i * 128 : (i + 1) * 128]
    acc[...] = jnp.zeros(acc.shape, F32)
    top[...] = jnp.full(top.shape, -1e30, F32)
    ready()

    for g in range(2):
        src = lambda g=g: w_hbm.at[:, f, pl.ds(96 * g, 96)]
        link.send(("w", g, "y"), src, lambda g=g: wp.at[:, f, pl.ds(96 * g, 96)], here.yhi)

    def send_tok(j, h):
        src = (0, 1, 3)[j], (0, 2, 4)[j]
        dst = (1, 3, 5)[j], (2, 4, 6)[j]
        link.send(("up", j, h), lambda: blocks.at[src[0], h], lambda: blocks.at[dst[0], h], here.zp)
        link.send(("down", j, h), lambda: blocks.at[src[1], h], lambda: blocks.at[dst[1], h], here.zm)

    def wait_tok(j, h):
        dst = (1, 3, 5)[j], (2, 4, 6)[j]
        link.wait(("up", j, h), lambda: blocks.at[dst[0], h], here.zm)
        link.wait(("down", j, h), lambda: blocks.at[dst[1], h], here.zp)

    send_tok(0, 0)
    send_tok(0, 1)
    for d, dev in enumerate(seq_peers):
        link.send(("mod", d + 1), lambda: modbuf.at[s], lambda: modbuf.at[s], dev)

    def slice_of(who, g, half=None):
        if half is None:
            return lambda: wp.at[:, who, pl.ds(96 * g, 96)]
        return lambda: wp.at[:, who, pl.ds(96 * g + 48 * half, 48)]

    def w_send(name, who, g, dev, half=None):
        link.send(("w", g, name), slice_of(who, g, half), slice_of(who, g, half), dev)

    def w_wait(name, who, g, half=None):
        link.wait(("w", g, name), slice_of(who, g, half), here.sib)

    def w_spread(y, g):
        who = here.frame_at(y, 0, 0)
        w_send((y, "xp"), who, g, here.xp)
        w_send((y, "xm"), who, g, here.xm)
        w_send((y, "s0"), who, g, here.sib)

    def w_begin(g):
        w_wait("y", f, g)
        w_send("ylo", f, g, here.ylo)
        w_spread(0, g)

    def w_second(g):
        w_wait("ylo", here.frame_at(1, 0, 0), g)
        w_spread(1, g)

    def w_relay(y, g):
        left, right = here.frame_at(y, 3, 0), here.frame_at(y, 1, 0)
        w_wait((y, "xp"), left, g)
        w_send((y, "xp2"), left, g, here.xp, 0)
        w_send((y, "s3"), left, g, here.sib)
        w_wait((y, "xm"), right, g)
        w_send((y, "xm2"), right, g, here.xm, 1)
        w_send((y, "s1"), right, g, here.sib)

    def w_finish(y, g):
        far = here.frame_at(y, 2, 0)
        w_wait((y, "xp2"), far, g, 0)
        w_wait((y, "xm2"), far, g, 1)
        w_send((y, "s2"), far, g, here.sib)

    def w_from_sib(y, g):
        for dx in range(4):
            w_wait((y, f"s{dx}"), here.frame_at(y, dx, 1), g)

    def wo_at(zz, c, h):
        return lambda: wz.at[zz, c, h]

    def wo_start():
        rows = pl.ds(pl.multiple_of(core * 64, 64), 64)
        for h in range(2):
            src = lambda h=h: wo_hbm.at[rows, pl.ds(h * 1536, 1536)]
            link.send(("wo", "up", 1, h), src, wo_at(z, core, h), here.zp)
            link.send(("wo", "down", 1, h), src, wo_at(z, core, h), here.zm)

    def wo_relay(d, h):
        for way, zz, dev, last in (("up", here.z_at(-d), here.zp, 0), ("down", here.z_at(d), here.zm, 1)):
            if d == 4 and h != last:
                continue
            at = wo_at(zz, core, h)
            link.wait(("wo", way, d, h), at, dev)
            if d < 3 or (d == 3 and h == last):
                link.send(("wo", way, d + 1, h), at, at, dev)
            link.send(("wo", "sib", way, d, h), at, at, here.sib)

    def wo_from_sib(d, h):
        for way, zz, last in (("up", here.z_at(-d), 0), ("down", here.z_at(d), 1)):
            if d == 4 and h != last:
                continue
            link.wait(("wo", "sib", way, d, h), wo_at(zz, 1 - core, h), here.sib)

    first = lax.broadcasted_iota(jnp.int32, (1, GROUP), 1) < HEAD
    q_scale = math.log2(math.e) / math.sqrt(HEAD)

    def normalise(raw):
        def tile(h, c):
            return raw[h, :, c * 128 : (c + 1) * 128].astype(F32)

        spots = [(h, c) for h in range(2) for c in range(6)]
        total = jnp.zeros((80, 128), F32)
        for h, c in spots:
            total = total + tile(h, c)
        mean = jnp.sum(total[:40] + total[40:], axis=-1, keepdims=True) * (1.0 / D)
        mean = jnp.concatenate([mean, mean], axis=0)
        total = jnp.zeros((80, 128), F32)
        for h, c in spots:
            diff = tile(h, c) - mean
            total = total + diff * diff
        var = jnp.sum(total[:40] + total[40:], axis=-1, keepdims=True) * (1.0 / D)
        inv = lax.rsqrt(var + 1e-05)
        inv = jnp.concatenate([inv, inv], axis=0)
        return lambda h, c: (tile(h, c) - mean) * inv

    def modulate(p, a, b):
        na, nb = normalise(blocks.at[a]), normalise(blocks.at[b])
        for h in range(2):
            for c in range(6):
                va, vb = na(h, c), nb(h, c)
                for half in range(2):
                    t = h * 12 + half * 6 + c
                    rows = slice(half * 40, half * 40 + 40)
                    both = jnp.concatenate([va[rows], vb[rows]], axis=0)
                    scale = 1.0 + modt[24 + t : 25 + t, :]
                    out = both * scale + modt[t : t + 1, :]
                    x_scr[p, t // 6, :, (t % 6) * 128 : (t % 6 + 1) * 128] = out.astype(BF)

    q_gain = jnp.concatenate([qg_ref[...]] * 2, axis=1) * q_scale
    k_gain = jnp.concatenate([kg_ref[...]] * 2, axis=1)

    def finish_qkv(qkv):
        q = head_norm_pair(qkv[:, :GROUP], q_gain, first)
        k = head_norm_pair(qkv[:, GROUP : 2 * GROUP], k_gain, first)
        return q.astype(BF), k.astype(BF), qkv[:, 2 * GROUP :].astype(BF)

    def project(p, n=1):
        rows = n * 80
        x = jnp.concatenate([x_scr[p : p + n, k].reshape(rows, 768) for k in range(4)], axis=1)
        sides = [side[j] for side in (wp, w_ref) for j in range(3)]
        for pair in range(3):
            part = jnp.concatenate([sides[2 * pair + i].reshape(D, GROUP) for i in range(2)], axis=1)
            joined[0:rows, pair * 256 : (pair + 1) * 256] = jnp.dot(
                x, part, preferred_element_type=F32
            )
        for i in range(n):
            keep_swap(p + i, *finish_qkv(joined[i * 80 : i * 80 + 80, : 3 * GROUP]))
            send_swap(p + i)
        for i in range(n):
            keep_own(p + i, *finish_qkv(joined[i * 80 : i * 80 + 80, 3 * GROUP :]))

    def put_q(p, half, q):
        row = p * 160 + half * 80
        none = jnp.zeros(q.shape, BF)
        qm[row : row + 80, :] = jnp.where(first, q, none)
        qm[640 + row : 720 + row, :] = jnp.where(first, none, q)

    def keep_own(p, q, k, v):
        put_q(p, 0, q)
        kv[p, 0, 0, 0, 0:80] = k
        kv[p, 0, 0, 1, 0:80] = v

    def keep_swap(p, q, k, v):
        swap[p, 0] = q
        swap[p, 1] = k
        swap[p, 2] = v

    def send_swap(p):
        link.send(
            ("kvswap", p),
            lambda: swap.at[p, pl.ds(1, 2)],
            lambda: kv.at[p, 0, 0, :, pl.ds(80, 80)],
            here.yhi,
        )
        link.send(("qswap", p), lambda: swap.at[p, 0], lambda: qin.at[p], here.yhi)

    def kv_from_y(p):
        link.wait(("kvswap", p), lambda: kv.at[p, 0, 0, :, pl.ds(80, 80)], here.yhi)

    def kv_at(p, x, j, kind=None):
        if kind is None:
            return lambda: kv.at[p, x, j]
        return lambda: kv.at[p, x, j, kind]

    def kv_send(p, src, dst, dev, kind=None):
        link.send(("kv", p, dst, kind), kv_at(p, *src, kind), kv_at(p, *dst, kind), dev)

    def kv_wait(p, dst, kind=None):
        link.wait(("kv", p, dst, kind), kv_at(p, *dst, kind), here.sib)

    def to_sib(p, x):
        src, dst = (lambda: kv.at[p, x, pl.ds(0, 2)]), (lambda: kv.at[p, x, pl.ds(2, 2)])
        link.send(("sib", p, x), src, dst, here.sib)

    def from_sib(p, x):
        link.wait(("sib", p, x), lambda: kv.at[p, x, pl.ds(2, 2)], here.sib)

    def spread(p, y):
        kv_send(p, (0, y), (1, y), here.xp)
        kv_send(p, (0, y), (2, y), here.xm)

    def begin(p):
        kv_from_y(p)
        kv_send(p, (0, 0), (0, 1), here.ylo)
        spread(p, 0)

    def arrive_y(p):
        kv_wait(p, (0, 1))
        spread(p, 1)
        to_sib(p, 0)

    def relay(p, y):
        kv_wait(p, (1, y))
        kv_send(p, (1, y), (3, y), here.xp, 0)
        kv_wait(p, (2, y))
        kv_send(p, (2, y), (3, y), here.xm, 1)
        if y == 1:
            to_sib(p, 1)
            to_sib(p, 2)

    def finish(p):
        for y in range(2):
            kv_wait(p, (3, y), 0)
            kv_wait(p, (3, y), 1)
        to_sib(p, 3)

    w_begin(0)
    w_begin(1)
    wait_tok(0, 0)
    send_tok(1, 0)
    w_second(0)
    w_relay(0, 0)
    wait_tok(0, 1)
    send_tok(1, 1)
    w_second(1)
    w_relay(0, 1)
    wait_tok(1, 0)
    send_tok(2, 0)
    w_relay(1, 0)
    for d in range(1, 16):
        peer = lax.rem(s + 16 - d, 16)
        link.wait(("mod", d), lambda: modbuf.at[peer], (f, peer))
    for i in range(8):
        low, high = modbuf[2 * i], modbuf[2 * i + 1]
        modt[9 * i : 9 * i + 4, :] = low[0:4]
        modt[9 * i + 4 : 9 * i + 5, :] = low[4:5] + high[0:1]
        modt[9 * i + 5 : 9 * i + 9, :] = high[1:5]
    modulate(1, 1, 2)
    wait_tok(1, 1)
    send_tok(2, 1)
    w_relay(1, 1)
    for g in range(2):
        w_finish(0, g)
    modulate(2, 3, 4)
    wait_tok(2, 0)
    link.send(("up", 3), lambda: blocks.at[5, 0], lambda: blocks.at[7, 0], here.zp)
    local[1].wait()
    for g in range(2):
        w_finish(1, g)
    for g in range(2):
        w_from_sib(0, g)
        w_from_sib(1, g)
    project(1, 2)

    wait_tok(2, 1)
    link.send(("down", 3), lambda: blocks.at[6, 1], lambda: blocks.at[7, 1], here.zm)
    modulate(3, 5, 6)
    project(3)
    begin(1)
    begin(2)
    link.wait(("up", 3), lambda: blocks.at[7, 0], here.zm)
    link.wait(("down", 3), lambda: blocks.at[7, 1], here.zp)
    wo_start()
    modulate(0, 0, 7)
    project(0)
    arrive_y(1)
    begin(3)
    for p in (1, 2, 3, 0):
        link.wait(("qswap", p), lambda p=p: qin.at[p], here.yhi)
        put_q(p, 1, qin[p])
    begin(0)

    upper = lax.broadcasted_iota(jnp.int32, (GROUP, 640), 0) < HEAD

    def attend(t):
        p, x = (t // 4 + 1) % 4, t % 4
        keys = kv[p, x, :, 0].reshape(640, GROUP)
        values = kv[p, x, :, 1].reshape(640, GROUP).T
        one = jnp.ones((GROUP, 640), BF)
        vt[0] = jnp.where(upper, values, one)
        vt[1] = jnp.where(upper, one, values)
        def score(n):
            s_scr[n % 2] = lax.dot_general(
                keys, qm[n * 128 : (n + 1) * 128, :], (((1,), (1,)), ((), ())),
                preferred_element_type=F32,
            )

        def weigh(n):
            cols = slice(n * 128, (n + 1) * 128)
            old = top[0:1, cols]
            new = jnp.maximum(old, jnp.max(s_scr[n % 2], axis=0, keepdims=True))
            p_scr[n % 2] = jnp.exp2(s_scr[n % 2] - new).astype(BF)
            top[0:1, cols] = new
            return jnp.exp2(old - new)

        def mix(n, shrink):
            cols = slice(n * 128, (n + 1) * 128)
            part = jnp.dot(vt[n // 5], p_scr[n % 2], preferred_element_type=F32)
            acc[:, cols] = acc[:, cols] * shrink + part

        score(0)
        shrink = None
        for n in range(10):
            if n < 9:
                score(n + 1)
            now = weigh(n)
            if n:
                mix(n - 1, shrink)
            shrink = now
        mix(9, shrink)

    def send_base():
        link.send("tok", lambda: blocks.at[0], lambda: nexttok, here.prev)
        link.send("gate", lambda: modt.at[pl.ds(48, 24)], lambda: nextgate, here.prev)

    events = {
        0: [(arrive_y, 2), (relay, 1, 0), (relay, 1, 1), (wo_relay, 1, 0)],
        1: [(relay, 2, 0), (wo_relay, 1, 1)],
        2: [(arrive_y, 3), (finish, 1)],
        3: [(relay, 2, 1)],
        4: [(arrive_y, 0), (relay, 3, 0), (wo_relay, 2, 0)],
        5: [(finish, 2), (relay, 3, 1)],
        6: [(relay, 0, 0), (wo_relay, 2, 1)],
        7: [(relay, 0, 1)],
        8: [(finish, 3)],
        9: [(wo_relay, 3, 0)],
        10: [(finish, 0)],
        12: [(wo_relay, 3, 1)],
        13: [(send_base,)],
        15: [(wo_relay, 4, 0), (wo_relay, 4, 1)],
    }
    for t in range(16):
        events.setdefault(t, []).append((from_sib, (t // 4 + 1) % 4, t % 4))

    def step(t, carry):
        for when, acts in events.items():

            @pl.when(t == when)
            def _():
                for act, *args in acts:
                    act(*args)

        attend(t)
        return carry

    lax.fori_loop(0, 16, step, 0)

    upper_part = acc[0:64, 0:640] * (1.0 / acc[64:65, 0:640])
    lower_part = acc[64:128, 640:1280] * (1.0 / acc[0:1, 640:1280])
    mixed[...] = jnp.concatenate([upper_part, lower_part], axis=0).T

    def rows_of(p, b):
        base = p * 160 + b * 40
        return jnp.concatenate([mixed[base : base + 40], mixed[base + 80 : base + 120]], axis=0).astype(BF)

    targets = [(0, 1)] + [(p, b) for p in (3, 2, 1) for b in (0, 1)]
    for i, (p, b) in enumerate(targets):
        outbox[i] = rows_of(p, b)
        dev = here.along_z((4 if p == 0 else p) if b else -p)
        link.send(("mix", i), lambda i=i: outbox.at[i], lambda: lhs.at[z], dev)
    lhs[z] = rows_of(0, 0)
    link.drain()
    for d in (1, 2, 3, 4):
        for h in range(2):
            wo_from_sib(d, h)
    for i, (p, b) in enumerate(targets):
        source = here.z_at((-4 if p == 0 else -p) if b else p)
        link.wait(("mix", i), lambda source=source: lhs.at[source], here.zp)

    for copy in local[2:]:
        copy.wait()

    left = jnp.concatenate([lhs[i] for i in range(8)], axis=1)
    for m in range(4):
        h, c = m // 2, (m % 2) * 768
        right = wz[:, :, h, :, c : c + 768].reshape(1024, 768)
        total = jnp.dot(left, right, preferred_element_type=F32)
        give[m] = jnp.concatenate([total[40:, :384], total[40:, 384:]], axis=0).astype(BF)
        link.send(("give", m), lambda m=m: give.at[m], lambda m=m: give_in.at[m], here.prev_y)
        keep[m] = jnp.concatenate([total[:40, :384], total[:40, 384:]], axis=0).astype(BF)
        link.send(("keep", m), lambda m=m: keep.at[m], lambda m=m: keep_in.at[m], here.prev)
    link.wait("tok", lambda: nexttok, here.next)
    link.wait("gate", lambda: nextgate, here.next)
    for m in range(4):
        h, k = m // 2, m % 2
        base = nexttok[h].astype(F32)[k * 40 : k * 40 + 40]
        link.wait(("keep", m), lambda m=m: keep_in.at[m], here.next)
        link.wait(("give", m), lambda m=m: give_in.at[m], here.next_y)
        total = keep_in[m].astype(F32) + give_in[m].astype(F32)
        for half in range(2):
            for c in range(3):
                t = m * 6 + half * 3 + c
                term = total[half * 40 : half * 40 + 40, c * 128 : (c + 1) * 128] * nextgate[t : t + 1, :]
                at = half * 384 + c * 128
                out_ref[:, t * 128 : (t + 1) * 128] = (base[:, at : at + 128] + term).astype(BF)
    link.drain()
    assert len(link.ids) <= N_COPIES, len(link.ids)


def layer_call(*operands):
    vm = pl.BlockSpec(memory_space=pltpu.VMEM)
    hbm = pl.BlockSpec(memory_space=pl.ANY)
    return pl.pallas_call(
        layer_kernel,
        out_shape=jax.ShapeDtypeStruct((TOK, D), BF),
        in_specs=[vm, vm, hbm, hbm, hbm, vm, vm],
        out_specs=vm,
        scratch_shapes=[
            pltpu.VMEM((576, TEMB), BF),
            pltpu.VMEM((3, 16, 192, GROUP), BF),
            pltpu.VMEM((8, 2, 80, 768), BF),
            pltpu.VMEM((16, 8, 128), F32),
            pltpu.VMEM((72, 128), F32),
            pltpu.VMEM((3, 16, 192, GROUP), BF),
            pltpu.VMEM((4, 4, 80, 768), BF),
            pltpu.VMEM((4, 3, 80, GROUP), BF),
            pltpu.VMEM((4, 80, GROUP), BF),
            pltpu.VMEM((4, 4, 4, 2, 160, GROUP), BF),
            pltpu.VMEM((1280, GROUP), BF),
            pltpu.VMEM((2, GROUP, 640), BF),
            pltpu.VMEM((GROUP, 1280), F32),
            pltpu.VMEM((8, 1280), F32),
            pltpu.VMEM((8, 2, 2, 64, 1536), BF),
            pltpu.VMEM((640, GROUP), F32),
            pltpu.VMEM((7, 80, GROUP), BF),
            pltpu.VMEM((8, 80, GROUP), BF),
            pltpu.VMEM((4, 80, 384), BF),
            pltpu.VMEM((4, 80, 384), BF),
            pltpu.VMEM((4, 80, 384), BF),
            pltpu.VMEM((4, 80, 384), BF),
            pltpu.VMEM((2, 80, 768), BF),
            pltpu.VMEM((24, 128), F32),
            pltpu.VMEM((2, 640, GROUP), F32),
            pltpu.VMEM((2, 640, GROUP), BF),
            pltpu.VMEM((160, 6 * GROUP), F32),
            pltpu.SemaphoreType.DMA((N_COPIES,)),
            pltpu.SemaphoreType.DMA((N_COPIES,)),
            pltpu.SemaphoreType.DMA((6,)),
        ],
        compiler_params=pltpu.CompilerParams(
            collective_id=0, has_side_effects=True, vmem_limit_bytes=VMEM_LIMIT
        ),
        name="layer",
    )(*operands)


def body(queue_tokens, timesteps, fresh_noise, w_mod, w_qkv, q_gain, k_gain, w_out):
    condition = jax.nn.silu(embed_steps(timesteps)).astype(BF)
    w = jnp.transpose(w_qkv, (1, 0, 2)).reshape(3, 16, 192, GROUP)
    arrived = layer_call(queue_tokens[0], condition, w_mod.T, w, w_out, q_gain[None], k_gain[None])
    last = lax.axis_index("frame") == lax.axis_size("frame") - 1
    return jnp.where(last, fresh_noise, arrived)[None]


def solution(mesh):
    return jax.shard_map(
        body,
        mesh=mesh,
        in_specs=(
            P("frame", "seq", None),
            P("frame"),
            P("seq", None),
            P(None, "seq"),
            P(None, None, "seq"),
            P(),
            P(),
            P("seq", None),
        ),
        out_specs=P("frame", "seq", None),
        check_vma=False,
    )
```

```python
import math

import jax
import jax.numpy as jnp
from jax import lax
from jax.experimental import pallas as pl
from jax.experimental.pallas import tpu as pltpu
from jax.sharding import PartitionSpec as P

TEMB = 512
TOK = 40
D = 3072
GROUP = 128
HEAD = 64
BF = jnp.bfloat16
F32 = jnp.float32
MESH = pl.DeviceIdType.MESH
VMEM_LIMIT = 56 * 1024 * 1024


def embed_steps(levels):
    halfway = TEMB // 2
    frequency = jnp.exp(-math.log(10000.0) * jnp.arange(halfway, dtype=F32) / halfway)
    angles = levels.astype(F32)[:, None] * frequency[None, :]
    return jnp.concatenate([jnp.cos(angles), jnp.sin(angles)], axis=-1)


class Place:
    def __init__(self):
        f = lax.axis_index("frame")
        s = lax.axis_index("seq")
        self.f, self.s = f, s
        ylo, x, core = f // 8, (f // 2) % 4, f % 2
        yhi, z = s // 8, s % 8
        self.core, self.z, self.yhi_at = core, z, yhi
        self.zs = {d: (z + d + 8) % 8 for d in range(-4, 5)}
        self.coords = (ylo, x, core)
        self.sib = (self.frame_at(0, 0, 1), s)
        self.ylo = (self.frame_at(1, 0, 0), s)
        self.xp = (self.frame_at(0, 1, 0), s)
        self.xm = (self.frame_at(0, 3, 0), s)
        self.zp = self.along_z(1)
        self.zm = self.along_z(-1)
        self.yhi = (f, (1 - yhi) * 8 + z)
        self.prev = ((f + 15) % 16, s)
        self.next = ((f + 1) % 16, s)
        self.prev_y = ((f + 15) % 16, self.yhi[1])
        self.next_y = ((f + 1) % 16, self.yhi[1])
        self.far = ((f + 15 + 2 * core) % 16, s)

    def frame_at(self, dy, dx, dc):
        ylo, x, core = self.coords
        return (ylo + dy) % 2 * 8 + (x + dx) % 4 * 2 + (core + dc) % 2

    def z_at(self, d):
        return self.zs[d]

    def along_z(self, d):
        return (self.f, self.yhi_at * 8 + self.z_at(d))


class Link:
    def __init__(self, send_sem, recv_sem):
        self.send_sem, self.recv_sem = send_sem, recv_sem
        self.ids = {}
        self.sent = []

    def _copy(self, name, src, dst, dev):
        i = self.ids.setdefault(name, len(self.ids))
        return pltpu.make_async_remote_copy(
            src_ref=src(),
            dst_ref=dst(),
            send_sem=self.send_sem.at[i],
            recv_sem=self.recv_sem.at[i],
            device_id=dev,
            device_id_type=MESH,
        )

    def send(self, name, src, dst, dev):
        self._copy(name, src, dst, dev).start()
        self.sent.append((name, src, dst, dev))

    def wait(self, name, dst, dev):
        self._copy(name, dst, dst, dev).wait_recv()

    def drain(self):
        for sent in self.sent:
            self._copy(*sent).wait_send()
        self.sent = []


def meet(devices):
    barrier = pltpu.get_barrier_semaphore()
    for dev in devices:
        pl.semaphore_signal(barrier, inc=1, device_id=dev, device_id_type=MESH)
    return lambda: pl.semaphore_wait(barrier, len(devices))


def to_block(rows):
    pieces = []
    for h in range(2):
        lo = rows[:, h * 1536 : h * 1536 + 768]
        hi = rows[:, h * 1536 + 768 : (h + 1) * 1536]
        pieces.append(jnp.concatenate([lo, hi], axis=0))
    return pieces


def head_norm_pair(x, gain, first):
    a = jnp.sum(jnp.where(first, x, 0.0), axis=-1, keepdims=True) * (1.0 / HEAD)
    b = jnp.sum(jnp.where(first, 0.0, x), axis=-1, keepdims=True) * (1.0 / HEAD)
    c = x - jnp.where(first, a, b)
    sq = c * c
    va = jnp.sum(jnp.where(first, sq, 0.0), axis=-1, keepdims=True) * (1.0 / HEAD)
    vb = jnp.sum(jnp.where(first, 0.0, sq), axis=-1, keepdims=True) * (1.0 / HEAD)
    return c * lax.rsqrt(jnp.where(first, va, vb) + 1e-06) * gain


N_COPIES = 200


def layer_kernel(
    tok_ref, cond_ref, wm_hbm, w_hbm, wo_hbm, qg_ref, kg_ref,
    out_ref,
    wm_ref, w_ref, blocks, modbuf, modt, wp, x_scr, swap, qin, kv, qm, vt, acc, top,
    wz, mixed, outbox, lhs, give, give_in, keep, keep_in, nexttok, nextgate, s_scr, p_scr,
    joined, send_sem, recv_sem, local_sem,
):
    here = Place()
    f, s, z, core = here.f, here.s, here.z, here.core
    seq_peers = [(f, lax.rem(s + d, 16)) for d in range(1, 16)]
    ready = meet(seq_peers + [here.sib, here.ylo, here.xp, here.xm, here.far, here.prev_y, here.next_y])
    link = Link(send_sem, recv_sem)

    local = [
        pltpu.make_async_copy(wm_hbm, wm_ref, local_sem.at[0]),
        pltpu.make_async_copy(w_hbm, w_ref, local_sem.at[1]),
    ]
    for c in range(2):
        for h in range(2):
            src = wo_hbm.at[pl.ds(c * 64, 64), pl.ds(h * 1536, 1536)]
            local.append(pltpu.make_async_copy(src, wz.at[z, c, h], local_sem.at[2 + 2 * c + h]))
    for copy in local:
        copy.start()
    tok = tok_ref[...].astype(F32)
    for h, piece in enumerate(to_block(tok)):
        blocks[0, h] = piece.astype(BF)
    local[0].wait()
    own = lax.dot_general(
        jnp.broadcast_to(cond_ref[...].astype(F32), (16, TEMB)).astype(BF), wm_ref[...], (((1,), (1,)), ((), ())), preferred_element_type=F32
    )[0:1]
    gap = jnp.zeros((1, 64), F32)
    even = jnp.concatenate([own, gap], axis=1)
    odd = jnp.concatenate([gap, own], axis=1)
    own = jnp.where(s % 2 == 0, even, odd)
    modbuf[s] = jnp.zeros((8, 128), F32)
    for i in range(5):
        modbuf[s, i : i + 1, :] = own[:, i * 128 : (i + 1) * 128]
    acc[...] = jnp.zeros(acc.shape, F32)
    top[...] = jnp.full(top.shape, -1e30, F32)
    ready()

    for g in range(2):
        src = lambda g=g: w_hbm.at[:, f, pl.ds(96 * g, 96)]
        link.send(("w", g, "y"), src, lambda g=g: wp.at[:, f, pl.ds(96 * g, 96)], here.yhi)

    def send_tok(j, h):
        src = (0, 1, 3)[j], (0, 2, 4)[j]
        dst = (1, 3, 5)[j], (2, 4, 6)[j]
        link.send(("up", j, h), lambda: blocks.at[src[0], h], lambda: blocks.at[dst[0], h], here.zp)
        link.send(("down", j, h), lambda: blocks.at[src[1], h], lambda: blocks.at[dst[1], h], here.zm)

    def wait_tok(j, h):
        dst = (1, 3, 5)[j], (2, 4, 6)[j]
        link.wait(("up", j, h), lambda: blocks.at[dst[0], h], here.zm)
        link.wait(("down", j, h), lambda: blocks.at[dst[1], h], here.zp)

    send_tok(0, 0)
    send_tok(0, 1)
    for d, dev in enumerate(seq_peers):
        link.send(("mod", d + 1), lambda: modbuf.at[s], lambda: modbuf.at[s], dev)

    def slice_of(who, g, half=None):
        if half is None:
            return lambda: wp.at[:, who, pl.ds(96 * g, 96)]
        return lambda: wp.at[:, who, pl.ds(96 * g + 48 * half, 48)]

    def w_send(name, who, g, dev, half=None):
        link.send(("w", g, name), slice_of(who, g, half), slice_of(who, g, half), dev)

    def w_wait(name, who, g, half=None):
        link.wait(("w", g, name), slice_of(who, g, half), here.sib)

    def w_spread(y, g):
        who = here.frame_at(y, 0, 0)
        w_send((y, "xp"), who, g, here.xp)
        w_send((y, "xm"), who, g, here.xm)
        w_send((y, "s0"), who, g, here.sib)

    def w_begin(g):
        w_wait("y", f, g)
        w_send("ylo", f, g, here.ylo)
        w_spread(0, g)

    def w_second(g):
        w_wait("ylo", here.frame_at(1, 0, 0), g)
        w_spread(1, g)

    def w_relay(y, g):
        left, right = here.frame_at(y, 3, 0), here.frame_at(y, 1, 0)
        w_wait((y, "xp"), left, g)
        w_send((y, "xp2"), left, g, here.xp, 0)
        w_send((y, "s3"), left, g, here.sib)
        w_wait((y, "xm"), right, g)
        w_send((y, "xm2"), right, g, here.xm, 1)
        w_send((y, "s1"), right, g, here.sib)

    def w_finish(y, g):
        far = here.frame_at(y, 2, 0)
        w_wait((y, "xp2"), far, g, 0)
        w_wait((y, "xm2"), far, g, 1)
        w_send((y, "s2"), far, g, here.sib)

    def w_from_sib(y, g):
        for dx in range(4):
            w_wait((y, f"s{dx}"), here.frame_at(y, dx, 1), g)

    def wo_at(zz, c, h):
        return lambda: wz.at[zz, c, h]

    def wo_start():
        rows = pl.ds(pl.multiple_of(core * 64, 64), 64)
        for h in range(2):
            src = lambda h=h: wo_hbm.at[rows, pl.ds(h * 1536, 1536)]
            link.send(("wo", "up", 1, h), src, wo_at(z, core, h), here.zp)
            link.send(("wo", "down", 1, h), src, wo_at(z, core, h), here.zm)

    def wo_relay(d, h):
        for way, zz, dev, last in (("up", here.z_at(-d), here.zp, 0), ("down", here.z_at(d), here.zm, 1)):
            if d == 4 and h != last:
                continue
            at = wo_at(zz, core, h)
            link.wait(("wo", way, d, h), at, dev)
            if d < 3 or (d == 3 and h == last):
                link.send(("wo", way, d + 1, h), at, at, dev)
            if d == 4:
                link.send(("wo", "sib", way, d), at, at, here.sib)
            elif h == 1:
                whole = lambda zz=zz: wz.at[zz, core]
                link.send(("wo", "sib", way, d), whole, whole, here.sib)

    def wo_from_sib(d, h):
        for way, zz, last in (("up", here.z_at(-d), 0), ("down", here.z_at(d), 1)):
            if d == 4 and h == last:
                link.wait(("wo", "sib", way, d), wo_at(zz, 1 - core, h), here.sib)
            if d < 4 and h == 1:
                link.wait(("wo", "sib", way, d), lambda zz=zz: wz.at[zz, 1 - core], here.sib)

    first = lax.broadcasted_iota(jnp.int32, (1, GROUP), 1) < HEAD
    q_scale = math.log2(math.e) / math.sqrt(HEAD)

    def normalise(raw):
        def tile(h, c):
            return raw[h, :, c * 128 : (c + 1) * 128].astype(F32)

        spots = [(h, c) for h in range(2) for c in range(6)]
        total = jnp.zeros((80, 128), F32)
        for h, c in spots:
            total = total + tile(h, c)
        mean = jnp.sum(total[:40] + total[40:], axis=-1, keepdims=True) * (1.0 / D)
        mean = jnp.concatenate([mean, mean], axis=0)
        total = jnp.zeros((80, 128), F32)
        for h, c in spots:
            diff = tile(h, c) - mean
            total = total + diff * diff
        var = jnp.sum(total[:40] + total[40:], axis=-1, keepdims=True) * (1.0 / D)
        inv = lax.rsqrt(var + 1e-05)
        inv = jnp.concatenate([inv, inv], axis=0)
        return lambda h, c: (tile(h, c) - mean) * inv

    def modulate(p, a, b):
        na, nb = normalise(blocks.at[a]), normalise(blocks.at[b])
        for h in range(2):
            for c in range(6):
                va, vb = na(h, c), nb(h, c)
                for half in range(2):
                    t = h * 12 + half * 6 + c
                    rows = slice(half * 40, half * 40 + 40)
                    both = jnp.concatenate([va[rows], vb[rows]], axis=0)
                    scale = 1.0 + modt[24 + t : 25 + t, :]
                    out = both * scale + modt[t : t + 1, :]
                    x_scr[p, t // 6, :, (t % 6) * 128 : (t % 6 + 1) * 128] = out.astype(BF)

    q_gain = jnp.concatenate([qg_ref[...]] * 2, axis=1) * q_scale
    k_gain = jnp.concatenate([kg_ref[...]] * 2, axis=1)

    def finish_qkv(qkv):
        q = head_norm_pair(qkv[:, :GROUP], q_gain, first)
        k = head_norm_pair(qkv[:, GROUP : 2 * GROUP], k_gain, first)
        return q.astype(BF), k.astype(BF), qkv[:, 2 * GROUP :].astype(BF)

    def project(p, n=1):
        rows = n * 80
        x = jnp.concatenate([x_scr[p : p + n, k].reshape(rows, 768) for k in range(4)], axis=1)
        sides = [side[j] for side in (wp, w_ref) for j in range(3)]
        for pair in range(3):
            part = jnp.concatenate([sides[2 * pair + i].reshape(D, GROUP) for i in range(2)], axis=1)
            joined[0:rows, pair * 256 : (pair + 1) * 256] = jnp.dot(
                x, part, preferred_element_type=F32
            )
        for i in range(n):
            keep_swap(p + i, *finish_qkv(joined[i * 80 : i * 80 + 80, : 3 * GROUP]))
            send_swap(p + i)
        for i in range(n):
            keep_own(p + i, *finish_qkv(joined[i * 80 : i * 80 + 80, 3 * GROUP :]))

    def put_q(p, half, q):
        row = p * 160 + half * 80
        none = jnp.zeros(q.shape, BF)
        qm[row : row + 80, :] = jnp.where(first, q, none)
        qm[640 + row : 720 + row, :] = jnp.where(first, none, q)

    def keep_own(p, q, k, v):
        put_q(p, 0, q)
        kv[p, 0, 0, 0, 0:80] = k
        kv[p, 0, 0, 1, 0:80] = v

    def keep_swap(p, q, k, v):
        swap[p, 0] = q
        swap[p, 1] = k
        swap[p, 2] = v

    def send_swap(p):
        link.send(
            ("kvswap", p),
            lambda: swap.at[p, pl.ds(1, 2)],
            lambda: kv.at[p, 0, 0, :, pl.ds(80, 80)],
            here.yhi,
        )
        link.send(("qswap", p), lambda: swap.at[p, 0], lambda: qin.at[p], here.yhi)

    def kv_from_y(p):
        link.wait(("kvswap", p), lambda: kv.at[p, 0, 0, :, pl.ds(80, 80)], here.yhi)

    def kv_at(p, x, j, kind=None):
        if kind is None:
            return lambda: kv.at[p, x, j]
        return lambda: kv.at[p, x, j, kind]

    def kv_send(p, src, dst, dev, kind=None):
        link.send(("kv", p, dst, kind), kv_at(p, *src, kind), kv_at(p, *dst, kind), dev)

    def kv_wait(p, dst, kind=None):
        link.wait(("kv", p, dst, kind), kv_at(p, *dst, kind), here.sib)

    def to_sib(p, x):
        src, dst = (lambda: kv.at[p, x, pl.ds(0, 2)]), (lambda: kv.at[p, x, pl.ds(2, 2)])
        link.send(("sib", p, x), src, dst, here.sib)

    def from_sib(p, x):
        link.wait(("sib", p, x), lambda: kv.at[p, x, pl.ds(2, 2)], here.sib)

    def spread(p, y):
        kv_send(p, (0, y), (1, y), here.xp)
        kv_send(p, (0, y), (2, y), here.xm)

    def begin(p):
        kv_from_y(p)
        kv_send(p, (0, 0), (0, 1), here.ylo)
        spread(p, 0)

    def arrive_y(p):
        kv_wait(p, (0, 1))
        spread(p, 1)
        to_sib(p, 0)

    def relay(p, y):
        kv_wait(p, (1, y))
        kv_send(p, (1, y), (3, y), here.xp, 0)
        kv_wait(p, (2, y))
        kv_send(p, (2, y), (3, y), here.xm, 1)
        if y == 1:
            to_sib(p, 1)
            to_sib(p, 2)

    def finish(p):
        for y in range(2):
            kv_wait(p, (3, y), 0)
            kv_wait(p, (3, y), 1)
        to_sib(p, 3)

    w_begin(0)
    w_begin(1)
    wait_tok(0, 0)
    send_tok(1, 0)
    w_second(0)
    w_relay(0, 0)
    wait_tok(0, 1)
    send_tok(1, 1)
    w_second(1)
    w_relay(0, 1)
    wait_tok(1, 0)
    send_tok(2, 0)
    w_relay(1, 0)
    for d in range(1, 16):
        peer = lax.rem(s + 16 - d, 16)
        link.wait(("mod", d), lambda: modbuf.at[peer], (f, peer))
    for i in range(8):
        low, high = modbuf[2 * i], modbuf[2 * i + 1]
        modt[9 * i : 9 * i + 4, :] = low[0:4]
        modt[9 * i + 4 : 9 * i + 5, :] = low[4:5] + high[0:1]
        modt[9 * i + 5 : 9 * i + 9, :] = high[1:5]
    modulate(1, 1, 2)
    wait_tok(1, 1)
    send_tok(2, 1)
    w_relay(1, 1)
    for g in range(2):
        w_finish(0, g)
    modulate(2, 3, 4)
    wait_tok(2, 0)
    link.send(("up", 3), lambda: blocks.at[5, 0], lambda: blocks.at[7, 0], here.zp)
    local[1].wait()
    for g in range(2):
        w_finish(1, g)
    for g in range(2):
        w_from_sib(0, g)
        w_from_sib(1, g)
    project(1, 2)

    wait_tok(2, 1)
    link.send(("down", 3), lambda: blocks.at[6, 1], lambda: blocks.at[7, 1], here.zm)
    modulate(3, 5, 6)
    project(3)
    begin(1)
    begin(2)
    link.wait(("up", 3), lambda: blocks.at[7, 0], here.zm)
    link.wait(("down", 3), lambda: blocks.at[7, 1], here.zp)
    wo_start()
    modulate(0, 0, 7)
    project(0)
    arrive_y(1)
    begin(3)
    for p in (1, 2, 3, 0):
        link.wait(("qswap", p), lambda p=p: qin.at[p], here.yhi)
        put_q(p, 1, qin[p])
    begin(0)

    upper = lax.broadcasted_iota(jnp.int32, (GROUP, 640), 0) < HEAD

    def attend(t):
        p, x = (t // 4 + 1) % 4, t % 4
        keys = kv[p, x, :, 0].reshape(640, GROUP)
        values = kv[p, x, :, 1].reshape(640, GROUP).T
        one = jnp.ones((GROUP, 640), BF)
        vt[0] = jnp.where(upper, values, one)
        vt[1] = jnp.where(upper, one, values)
        def score(n):
            s_scr[n % 2] = lax.dot_general(
                keys, qm[n * 128 : (n + 1) * 128, :], (((1,), (1,)), ((), ())),
                preferred_element_type=F32,
            )

        def weigh(n):
            cols = slice(n * 128, (n + 1) * 128)
            old = top[0:1, cols]
            new = jnp.maximum(old, jnp.max(s_scr[n % 2], axis=0, keepdims=True))
            p_scr[n % 2] = jnp.exp2(s_scr[n % 2] - new).astype(BF)
            top[0:1, cols] = new
            return jnp.exp2(old - new)

        def mix(n, shrink):
            cols = slice(n * 128, (n + 1) * 128)
            part = jnp.dot(vt[n // 5], p_scr[n % 2], preferred_element_type=F32)
            acc[:, cols] = acc[:, cols] * shrink + part

        score(0)
        shrink = None
        for n in range(10):
            if n < 9:
                score(n + 1)
            now = weigh(n)
            if n:
                mix(n - 1, shrink)
            shrink = now
        mix(9, shrink)

    def send_base():
        link.send("tok", lambda: blocks.at[0], lambda: nexttok, here.prev)
        link.send("gate", lambda: modt.at[pl.ds(48, 24)], lambda: nextgate, here.prev)

    events = {
        0: [(arrive_y, 2), (relay, 1, 0), (relay, 1, 1), (wo_relay, 1, 0)],
        1: [(relay, 2, 0), (wo_relay, 1, 1)],
        2: [(arrive_y, 3), (finish, 1)],
        3: [(relay, 2, 1)],
        4: [(arrive_y, 0), (relay, 3, 0), (wo_relay, 2, 0)],
        5: [(finish, 2), (relay, 3, 1)],
        6: [(relay, 0, 0), (wo_relay, 2, 1)],
        7: [(relay, 0, 1)],
        8: [(finish, 3)],
        9: [(wo_relay, 3, 0)],
        10: [(finish, 0)],
        12: [(wo_relay, 3, 1)],
        13: [(send_base,)],
        15: [(wo_relay, 4, 0), (wo_relay, 4, 1)],
    }
    for t in range(16):
        events.setdefault(t, []).append((from_sib, (t // 4 + 1) % 4, t % 4))

    def step(t, carry):
        for when, acts in events.items():

            @pl.when(t == when)
            def _():
                for act, *args in acts:
                    act(*args)

        attend(t)
        return carry

    lax.fori_loop(0, 16, step, 0)

    upper_part = acc[0:64, 0:640] * (1.0 / acc[64:65, 0:640])
    lower_part = acc[64:128, 640:1280] * (1.0 / acc[0:1, 640:1280])
    mixed[...] = jnp.concatenate([upper_part, lower_part], axis=0).T

    def rows_of(p, b):
        base = p * 160 + b * 40
        return jnp.concatenate([mixed[base : base + 40], mixed[base + 80 : base + 120]], axis=0).astype(BF)

    targets = [(0, 1)] + [(p, b) for p in (3, 2, 1) for b in (0, 1)]
    for i, (p, b) in enumerate(targets):
        outbox[i] = rows_of(p, b)
        dev = here.along_z((4 if p == 0 else p) if b else -p)
        link.send(("mix", i), lambda i=i: outbox.at[i], lambda: lhs.at[z], dev)
    lhs[z] = rows_of(0, 0)
    link.drain()
    for d in (1, 2, 3, 4):
        for h in range(2):
            wo_from_sib(d, h)
    for i, (p, b) in enumerate(targets):
        source = here.z_at((-4 if p == 0 else -p) if b else p)
        link.wait(("mix", i), lambda source=source: lhs.at[source], here.zp)

    for copy in local[2:]:
        copy.wait()

    left = jnp.concatenate([lhs[i] for i in range(8)], axis=1)
    for m in range(4):
        h, c = m // 2, (m % 2) * 768
        right = wz[:, :, h, :, c : c + 768].reshape(1024, 768)
        total = jnp.dot(left, right, preferred_element_type=F32)
        give[m] = jnp.concatenate([total[40:, :384], total[40:, 384:]], axis=0).astype(BF)
        link.send(("give", m), lambda m=m: give.at[m], lambda m=m: give_in.at[m], here.prev_y)
        keep[m] = jnp.concatenate([total[:40, :384], total[:40, 384:]], axis=0).astype(BF)
        link.send(("keep", m), lambda m=m: keep.at[m], lambda m=m: keep_in.at[m], here.prev)
    link.wait("tok", lambda: nexttok, here.next)
    link.wait("gate", lambda: nextgate, here.next)
    for m in range(4):
        h, k = m // 2, m % 2
        base = nexttok[h].astype(F32)[k * 40 : k * 40 + 40]
        link.wait(("keep", m), lambda m=m: keep_in.at[m], here.next)
        link.wait(("give", m), lambda m=m: give_in.at[m], here.next_y)
        total = keep_in[m].astype(F32) + give_in[m].astype(F32)
        for half in range(2):
            for c in range(3):
                t = m * 6 + half * 3 + c
                term = total[half * 40 : half * 40 + 40, c * 128 : (c + 1) * 128] * nextgate[t : t + 1, :]
                at = half * 384 + c * 128
                out_ref[:, t * 128 : (t + 1) * 128] = (base[:, at : at + 128] + term).astype(BF)
    link.drain()
    assert len(link.ids) <= N_COPIES, len(link.ids)


def layer_call(*operands):
    vm = pl.BlockSpec(memory_space=pltpu.VMEM)
    hbm = pl.BlockSpec(memory_space=pl.ANY)
    return pl.pallas_call(
        layer_kernel,
        out_shape=jax.ShapeDtypeStruct((TOK, D), BF),
        in_specs=[vm, vm, hbm, hbm, hbm, vm, vm],
        out_specs=vm,
        scratch_shapes=[
            pltpu.VMEM((576, TEMB), BF),
            pltpu.VMEM((3, 16, 192, GROUP), BF),
            pltpu.VMEM((8, 2, 80, 768), BF),
            pltpu.VMEM((16, 8, 128), F32),
            pltpu.VMEM((72, 128), F32),
            pltpu.VMEM((3, 16, 192, GROUP), BF),
            pltpu.VMEM((4, 4, 80, 768), BF),
            pltpu.VMEM((4, 3, 80, GROUP), BF),
            pltpu.VMEM((4, 80, GROUP), BF),
            pltpu.VMEM((4, 4, 4, 2, 160, GROUP), BF),
            pltpu.VMEM((1280, GROUP), BF),
            pltpu.VMEM((2, GROUP, 640), BF),
            pltpu.VMEM((GROUP, 1280), F32),
            pltpu.VMEM((8, 1280), F32),
            pltpu.VMEM((8, 2, 2, 64, 1536), BF),
            pltpu.VMEM((640, GROUP), F32),
            pltpu.VMEM((7, 80, GROUP), BF),
            pltpu.VMEM((8, 80, GROUP), BF),
            pltpu.VMEM((4, 80, 384), BF),
            pltpu.VMEM((4, 80, 384), BF),
            pltpu.VMEM((4, 80, 384), BF),
            pltpu.VMEM((4, 80, 384), BF),
            pltpu.VMEM((2, 80, 768), BF),
            pltpu.VMEM((24, 128), F32),
            pltpu.VMEM((2, 640, GROUP), F32),
            pltpu.VMEM((2, 640, GROUP), BF),
            pltpu.VMEM((160, 6 * GROUP), F32),
            pltpu.SemaphoreType.DMA((N_COPIES,)),
            pltpu.SemaphoreType.DMA((N_COPIES,)),
            pltpu.SemaphoreType.DMA((6,)),
        ],
        compiler_params=pltpu.CompilerParams(
            collective_id=0, has_side_effects=True, vmem_limit_bytes=VMEM_LIMIT
        ),
        name="layer",
    )(*operands)


def body(queue_tokens, timesteps, fresh_noise, w_mod, w_qkv, q_gain, k_gain, w_out):
    condition = jax.nn.silu(embed_steps(timesteps)).astype(BF)
    w = jnp.transpose(w_qkv, (1, 0, 2)).reshape(3, 16, 192, GROUP)
    arrived = layer_call(queue_tokens[0], condition, w_mod.T, w, w_out, q_gain[None], k_gain[None])
    last = lax.axis_index("frame") == lax.axis_size("frame") - 1
    return jnp.where(last, fresh_noise, arrived)[None]


def solution(mesh):
    return jax.shard_map(
        body,
        mesh=mesh,
        in_specs=(
            P("frame", "seq", None),
            P("frame"),
            P("seq", None),
            P(None, "seq"),
            P(None, None, "seq"),
            P(),
            P(),
            P("seq", None),
        ),
        out_specs=P("frame", "seq", None),
        check_vma=False,
    )
```
